32 devices in a mesh: groups: 2 (over x), dp: 8 (over z, y), tensor: 2 (over core).
Axes of the slice: x: 2, y: 2, z: 4, core: 2. Of those that a mesh axis runs over, the one named last changes fastest.
Arguments:
- patches: bfloat16 [2048, 1280], P(('groups', 'dp')), parts along dimension 0, may hold values from -6 to 6
- image_tokens: int32 [16, 4], P(('groups', 'dp')), parts along dimension 0, may hold values from 1 to 16, 32 in all within a row
- vit_gain: float32 [1280], replicated, may hold values from 0.5 to 1.5
- vit_q: bfloat16 [1280, 1280], P(None, 'tensor'), may hold values from -0.15625 to 0.15625
- vit_k: bfloat16 [1280, 1280], P(None, 'tensor'), may hold values from -0.15625 to 0.15625
- vit_v: bfloat16 [1280, 1280], P(None, 'tensor'), may hold values from -0.15625 to 0.15625
- vit_out: bfloat16 [1280, 1280], P('tensor'), may hold values from -0.15625 to 0.15625
- merge_gain: float32 [1280], replicated, may hold values from 0.5 to 1.5
- merger_out: bfloat16 [5120, 8192], P('tensor', 'dp'), may hold values from -0.078125 to 0.078125
- text_rows: bfloat16 [2048, 8192], P(('groups', 'dp')), parts along dimension 0, may hold values from -6 to 6
- text_query: bfloat16 [2048, 4096], P(('groups', 'dp'), 'tensor'), parts along dimension 0, may hold values from -6 to 6
- text_seg: int32 [16, 128], P(('groups', 'dp')), parts along dimension 0, may hold values from 0 to 3, never falling along the last dimension, each value on 1 to 64 neighbouring positions
- vis_route: int32 [512, 1], P('groups'), parts along dimension 0, may hold values from 0 to 7; in each aligned block of 32 rows (0 to 31, 32 to 63, ...) at most 8 rows name the same one
- vis_seq: int32 [512], P('groups'), parts along dimension 0, may hold values from 0 to 3
- llm_gain: float32 [8192], replicated, may hold values from 0.5 to 1.5
- llm_k: bfloat16 [8192, 512], P('dp', 'tensor'), may hold values from -0.0625 to 0.0625
- llm_v: bfloat16 [8192, 512], P('dp', 'tensor'), may hold values from -0.0625 to 0.0625
Outputs:
- attended: bfloat16 [2048, 4096], P(('groups', 'dp'), 'tensor'), parts along dimension 0
The draws below stay inside these ranges and needn't reach their ends.
There are 2 independent parts, one for each index of `groups`. The reference program is written for one: setup_inputs(seed, part) draws one part's arguments, and reference() takes and returns one part's arrays. A program takes and returns all parts, laid end to end along the dimension named above; an argument that names none is the same for every part. Nothing has to cross between parts.
Inputs may be any that keep to these rules, and one draw needn't show every extreme that they name: `image_tokens`: each row sums to 32, so the images of a block fill its 128 patch rows exactly. `text_seg`: within a row the sequence number never falls, and every one of the 4 sequences has a text token. `vis_route`: among the rows of one index of dp (aligned blocks of 32 rows) at most 8 name the same owner, a bound that some block reaches of them.
All inputs are finite; a program needn't handle non-finite values.
Results may differ from the reference program's by a relative error of at most 0.015.
Values may be sent and summed in bfloat16 or wider, within the bound.
A program may use at most 64 MiB of HBM per device.

```python
import math
from functools import partial
import jax
import jax.numpy as jnp
import numpy as np
from jax import lax

VHD = 80
VW = 1280
MW = 5120
D = 8192
QH = 32
KVH = 4
HD = 128
QW = 4096
KW = 512
IMG_DEV = 4
MERGED_DEV = 32
TEXT = 128
SEQ_DEV = 4
PATCH_DEV = 128
CAP = 8
PATCHES = 1024
VTOK = 256
TEXTS = 1024
N_DP = 8


def with_ends(drawn, stream_key, least, high):
    extent = drawn.shape
    place = [jax.random.randint(jax.random.fold_in(stream_key, axis), (), 0, extent[axis]) for axis in range(len(extent))]
    drawn = drawn.at[tuple(place)].set(least)
    longest = extent.index(max(extent))
    place[longest] = (place[longest] + 1) % extent[longest]
    return drawn.at[tuple(place)].set(high)


def level_of(key, dims, pieces, smallest, high):
    loudness, own = 1.0, jax.random.fold_in(key, 6)
    for dim, blocks in pieces:
        steps = jnp.exp(jax.random.uniform(jax.random.fold_in(own, dim), (blocks,), jnp.float32, smallest / len(pieces), high / len(pieces)))
        loudness = loudness * jnp.repeat(steps, dims[dim] // blocks).reshape([-1 if axis == dim else 1 for axis in range(len(dims))])
    return loudness


def profile(count, total, bound, lean):
    portions = [(1 << 20) // math.isqrt(rank ** lean) + 1 for rank in range(2, count + 1)]
    rest, holding = total - bound - (count - 1), [1] * (count - 1)
    while rest > 0:
        movable = [i for i in range(count - 1) if holding[i] < bound]
        whole, remaining = sum([portions[i] for i in movable]), rest
        for i in movable:
            more = min(bound - holding[i], max(1, remaining * portions[i] // whole), rest)
            holding[i] = holding[i] + more
            rest = rest - more
    return np.array([bound] + holding)


def ragged_sizes(rng, number_of, total, most, slope):
    if number_of == 2:
        one = jax.random.randint(rng, (), max(1, total - most), min(most, total - 1) + 1)
        return jnp.stack([one, total - one])
    sizes = jnp.asarray(profile(number_of, total, most, slope), jnp.int32)
    twos = (number_of - 1) // 2
    donor, sink = sizes[1:1 + 2 * twos:2], sizes[2:2 + 2 * twos:2]
    slack = jnp.minimum(donor - 1, most - sink)
    shifted = jax.random.randint(jax.random.fold_in(rng, 1), (twos,), 0, 1 << 20) % (slack + 1)
    sizes = sizes.at[1:1 + 2 * twos:2].set(donor - shifted).at[2:2 + 2 * twos:2].set(sink + shifted)
    return sizes[jax.random.permutation(jax.random.fold_in(rng, 2), number_of)]


def assign_block(rng, own, number, rows, number_of, top, reach, lean):
    sequence = jax.random.permutation(rng, number_of)
    packed, ordinary = portions_of(number_of, rows * top, reach, lean, True), portions_of(number_of, rows * top, reach, lean, False)
    places = jnp.arange(number_of)

    def named(lengths, turn):
        used = int((lengths > 0).sum())
        fixed = max(1, used // 4)
        passed = fixed + (places - fixed + turn * (used - fixed)) % max(1, number_of - fixed)
        return jnp.zeros((number_of,), jnp.int32).at[sequence[jnp.where(places < fixed, places, passed)]].set(jnp.asarray(lengths, jnp.int32))

    lengths = jnp.where(number % 4 == 0, named(packed, number // 4), named(ordinary, number - number // 4 - 1))
    mixed = jax.random.permutation(jax.random.fold_in(own, 3), number_of)
    source_of, sink = mixed[0:number_of // 2 * 2:2], mixed[1:number_of // 2 * 2:2]
    room = jnp.minimum(lengths[source_of] - 1, reach - lengths[sink]) // 2
    room = jnp.where((source_of == sequence[0]) | (sink == sequence[0]) | (lengths[sink] == 0), 0, jnp.maximum(room, 0))
    passed = jax.random.randint(jax.random.fold_in(own, 4), (number_of // 2,), 0, 1 << 20) % (room + 1)
    lengths = lengths.at[source_of].add(-passed).at[sink].add(passed)
    labels = jnp.searchsorted(jnp.cumsum(lengths), jnp.arange(rows * top), side="right").astype(jnp.int32)
    grid = labels.reshape(top, rows).T
    grid = grid[jax.random.permutation(jax.random.fold_in(own, 1), rows)]
    turn = jax.random.randint(jax.random.fold_in(own, 2), (rows, 1), 0, top)
    return jnp.take_along_axis(grid, (jnp.arange(top)[None, :] + turn) % top, axis=1)


def portions_of(amount, total, bound, lean, full):
    loads = [(1 << 20) // math.isqrt(grade ** lean) + 1 for grade in range(1, amount + 1)]
    largest = bound if full else min(bound, max(-(-total // amount), total * loads[0] // sum(loads)))
    least = 1 if total - largest >= amount - 1 else 0
    holding, surplus = [largest] + [least] * (amount - 1), total - largest - least * (amount - 1)
    while surplus > 0:
        candidates = [i for i in range(1, amount) if holding[i] < largest] or [i for i in range(1, amount) if holding[i] < bound]
        whole, remaining = sum([loads[i] for i in candidates]), surplus
        for i in candidates:
            extra = min(bound - holding[i], max(1, remaining * loads[i] // whole), surplus)
            holding[i] = holding[i] + extra
            surplus = surplus - extra
    return np.array(holding)


def bell_draw(rng, extent, scale, most, split=(), held_as=jnp.bfloat16):
    values = jax.random.normal(rng, extent, jnp.float32) * scale
    if len(split) > 0:
        values = level_of(rng, extent, split, -0.22, 0.18) * values
    return jnp.clip(values, min=-most, max=most).astype(held_as)


def setup_inputs(seed: int = 0, part: int = 0) -> dict:
    arg_keys = jax.random.split(jax.random.key(seed), 18)
    own_keys = jax.random.split(jax.random.fold_in(arg_keys[17], part), 18)
    patches = bell_draw(own_keys[0], (PATCHES, VW), 1.0, 6.0, ((0, 8),))
    image_tokens = jax.vmap(lambda own: ragged_sizes(own, IMG_DEV, MERGED_DEV, MERGED_DEV // 2, 2))(jax.random.split(own_keys[1], N_DP)).reshape((N_DP, IMG_DEV)).astype(jnp.int32)
    vit_gain = jnp.clip(1.0 + 0.1 * jax.random.normal(arg_keys[2], (VW,), jnp.float32), 0.5, 1.5)
    vit_q = bell_draw(arg_keys[3], (VW, VW), VW ** -0.5, 0.15625, ((1, 2),))
    vit_k = bell_draw(arg_keys[4], (VW, VW), VW ** -0.5, 0.15625, ((1, 2),))
    vit_v = bell_draw(arg_keys[5], (VW, VW), VW ** -0.5, 0.15625, ((1, 2),))
    vit_out = bell_draw(arg_keys[6], (VW, VW), VW ** -0.5, 0.15625, ((0, 2),))
    merge_gain = jnp.clip(1.0 + 0.1 * jax.random.normal(arg_keys[7], (VW,), jnp.float32), 0.5, 1.5)
    merger_out = bell_draw(arg_keys[8], (MW, D), MW ** -0.5, 0.078125, ((0, 2), (1, 8)))
    text_rows = bell_draw(own_keys[9], (TEXTS, D), 1.0, 6.0, ((0, 8),))
    text_query = bell_draw(own_keys[10], (TEXTS, QW), 1.0, 6.0, ((0, 8), (1, 2)))
    text_seg = jax.vmap(lambda own: jnp.searchsorted(jnp.cumsum(ragged_sizes(own, SEQ_DEV, TEXT, TEXT // 2, 0)), jnp.arange(TEXT), side="right"))(jax.random.split(own_keys[11], N_DP)).reshape((N_DP, TEXT)).astype(jnp.int32)
    vis_route_keys = jax.random.split(jax.random.fold_in(own_keys[12], 1), VTOK // MERGED_DEV)
    vis_route_turns = jax.random.permutation(jax.random.fold_in(own_keys[12], 3), VTOK // MERGED_DEV)
    vis_route = jax.vmap(lambda own, number: assign_block(jax.random.fold_in(own_keys[12], 2), own, number, MERGED_DEV, N_DP, 1, CAP, 2))(vis_route_keys, vis_route_turns).reshape((VTOK, 1))
    vis_seq = with_ends(jax.random.randint(own_keys[13], (VTOK,), 0, SEQ_DEV), jax.random.fold_in(own_keys[13], 1), 0, SEQ_DEV - 1).astype(jnp.int32)
    llm_gain = jnp.clip(1.0 + 0.1 * jax.random.normal(arg_keys[14], (D,), jnp.float32), 0.5, 1.5)
    llm_k = bell_draw(arg_keys[15], (D, KW), D ** -0.5, 0.0625, ((0, 8), (1, 2)))
    llm_v = bell_draw(arg_keys[16], (D, KW), D ** -0.5, 0.0625, ((0, 8), (1, 2)))
    return {"patches": patches, "image_tokens": image_tokens, "vit_gain": vit_gain, "vit_q": vit_q, "vit_k": vit_k, "vit_v": vit_v, "vit_out": vit_out, "merge_gain": merge_gain, "merger_out": merger_out, "text_rows": text_rows, "text_query": text_query, "text_seg": text_seg, "vis_route": vis_route, "vis_seq": vis_seq, "llm_gain": llm_gain, "llm_k": llm_k, "llm_v": llm_v}


EPSILON = 1e-06
NEG_LARGE = -1e+30

def layer_norm(values, scale_gain):
    values = values.astype(jnp.float32)
    centred = values - lax.optimization_barrier(jnp.mean(values, axis=-1, keepdims=True))
    spread = lax.optimization_barrier(jnp.mean(centred * centred, axis=-1, keepdims=True))
    return centred * lax.rsqrt(spread + EPSILON) * scale_gain.astype(jnp.float32)

def rms_norm(values, scale_gain):
    values = values.astype(jnp.float32)
    power = lax.optimization_barrier(jnp.mean(values * values, axis=-1, keepdims=True))
    return values * lax.rsqrt(power + EPSILON) * scale_gain.astype(jnp.float32)

def image_index(counts, total):
    ends = 4 * jnp.cumsum(counts.astype(jnp.int32))
    positions = jnp.arange(total, dtype=jnp.int32)
    return lax.optimization_barrier(jnp.sum((positions[:, None] >= ends[None, :]).astype(jnp.int32), axis=1))

def local_attention(query, keys, values, allowed, scale):
    scores = jnp.einsum('tagd,kad->agtk', query.astype(jnp.float32), keys.astype(jnp.float32)) * scale
    scores = jnp.where(allowed[None, None], scores, NEG_LARGE)
    weights = lax.optimization_barrier(jax.nn.softmax(scores, axis=-1).astype(jnp.bfloat16))
    mixed = jnp.einsum('agtk,kad->tagd', weights.astype(jnp.float32), values.astype(jnp.float32))
    return mixed.reshape(query.shape[0], -1).astype(jnp.bfloat16)

def head_split(inputs, weight, size):
    product = jnp.dot(inputs, weight, preferred_element_type=jnp.float32).astype(jnp.bfloat16)
    return product.reshape(inputs.shape[0], -1, size)

def vision_device(operands, vit_gain, vit_q, vit_k, vit_v, vit_out, merge_gain):
    patch_rows, counts = operands
    total = patch_rows.shape[0]
    image_of = image_index(counts, total)
    same_image = image_of[:, None] == image_of[None, :]
    normed = layer_norm(patch_rows, vit_gain).astype(jnp.bfloat16)
    vision_query = head_split(normed, vit_q, VHD)[:, :, None, :]
    vision_key = head_split(normed, vit_k, VHD)
    vision_value = head_split(normed, vit_v, VHD)
    attended = local_attention(vision_query, vision_key, vision_value, same_image, 1.0 / math.sqrt(VHD))
    mixed = jnp.dot(attended, vit_out, preferred_element_type=jnp.float32)
    hidden = (patch_rows.astype(jnp.float32) + mixed).astype(jnp.bfloat16)
    merged = layer_norm(hidden, merge_gain).astype(jnp.bfloat16)
    return merged.reshape(total // 4, 4 * VW)

def owner_attention(operands, visual_key, visual_value, route, visual_seq):
    query, text_key, text_value, segment, owner = operands
    length = query.shape[0]
    positions = jnp.arange(length, dtype=jnp.int32)
    text_allowed = (segment[:, None] == segment[None, :]) & (positions[None, :] <= positions[:, None])
    visual_allowed = (route[None, :] == owner) & (visual_seq[None, :] == segment[:, None])
    allowed = jnp.concatenate([visual_allowed, text_allowed], axis=1)
    query_heads = query.reshape(length, KVH, QH // KVH, HD)
    all_keys = jnp.concatenate([visual_key, text_key], axis=0).reshape(-1, KVH, HD)
    all_values = jnp.concatenate([visual_value, text_value], axis=0).reshape(-1, KVH, HD)
    return local_attention(query_heads, all_keys, all_values, allowed, 1.0 / math.sqrt(HD))

def reference(patches, image_tokens, vit_gain, vit_q, vit_k, vit_v, vit_out, merge_gain, merger_out, text_rows, text_query, text_seg, vis_route, vis_seq, llm_gain, llm_k, llm_v):
    vision = partial(vision_device, vit_gain=vit_gain, vit_q=vit_q, vit_k=vit_k, vit_v=vit_v, vit_out=vit_out, merge_gain=merge_gain)
    merged = lax.map(vision, (patches.reshape(N_DP, PATCH_DEV, VW), image_tokens))
    merged = merged.reshape(N_DP * MERGED_DEV, MW)
    projected = jnp.dot(merged, merger_out, preferred_element_type=jnp.float32).astype(jnp.bfloat16)
    text_in = rms_norm(text_rows, llm_gain).astype(jnp.bfloat16)
    visual_in = rms_norm(projected, llm_gain).astype(jnp.bfloat16)
    text_key = jnp.dot(text_in, llm_k, preferred_element_type=jnp.float32).astype(jnp.bfloat16)
    text_value = jnp.dot(text_in, llm_v, preferred_element_type=jnp.float32).astype(jnp.bfloat16)
    visual_key = jnp.dot(visual_in, llm_k, preferred_element_type=jnp.float32).astype(jnp.bfloat16)
    visual_value = jnp.dot(visual_in, llm_v, preferred_element_type=jnp.float32).astype(jnp.bfloat16)
    attend = partial(owner_attention, visual_key=visual_key, visual_value=visual_value, route=vis_route[:, 0], visual_seq=vis_seq)
    owners = jnp.arange(N_DP, dtype=jnp.int32)
    result = lax.map(attend, (text_query.reshape(N_DP, TEXT, QW), text_key.reshape(N_DP, TEXT, KW), text_value.reshape(N_DP, TEXT, KW), text_seg, owners))
    return result.reshape(N_DP * TEXT, QW)
```

```python
import functools
import math

import jax
import jax.numpy as jnp
from jax import lax
from jax.experimental import pallas as pl
from jax.experimental.pallas import tpu as pltpu
from jax.sharding import PartitionSpec as P

VHD = 80
QH = 32
KVH = 4
HD = 128


EPSILON = 1e-06
NEG_LARGE = -1e30


def layer_norm(values, scale_gain):
    values = values.astype(jnp.float32)
    centred = values - jnp.mean(values, axis=-1, keepdims=True)
    spread = jnp.mean(centred * centred, axis=-1, keepdims=True)
    return centred * lax.rsqrt(spread + EPSILON) * scale_gain


def rms_norm(values, scale_gain):
    values = values.astype(jnp.float32)
    power = jnp.mean(values * values, axis=-1, keepdims=True)
    return values * lax.rsqrt(power + EPSILON) * scale_gain


def image_index(counts, total):
    ends = 4 * jnp.cumsum(counts)
    positions = jnp.arange(total, dtype=jnp.int32)
    return jnp.sum((positions[:, None] >= ends[None, :]).astype(jnp.int32), axis=1)


def local_attention(query, keys, values, allowed, scale):
    scores = jnp.einsum("tagd,kad->agtk", query, keys, preferred_element_type=jnp.float32) * scale
    scores = jnp.where(allowed[None, None], scores, NEG_LARGE)
    weights = jax.nn.softmax(scores, axis=-1).astype(jnp.bfloat16)
    mixed = jnp.einsum("agtk,kad->tagd", weights, values, preferred_element_type=jnp.float32)
    return mixed.reshape(query.shape[0], -1).astype(jnp.bfloat16)


MESH = pl.DeviceIdType.MESH
MARK = 128


def dot32(left, right):
    return jnp.dot(left, right, preferred_element_type=jnp.float32)


def kernel(
    n,
    patches,
    image_col,
    image_row,
    vit_gain,
    vit_q_hbm,
    vit_k_hbm,
    vit_v_hbm,
    vit_out_hbm,
    merge_gain,
    merger_hbm,
    text_hbm,
    selector,
    llm_gain,
    llm_k_hbm,
    llm_v_hbm,
    out,
    wq,
    wk,
    wv,
    wo,
    merger,
    pair_weight,
    text,
    text_in,
    text_buf,
    query,
    keys,
    values,
    mixed,
    mix,
    mix_recv,
    merged,
    part,
    part_recv,
    text_send,
    text_recv,
    vis_send,
    vis_recv,
    load_sem,
    text_sems,
    forward_sems,
    mix_sems,
    merged_sems,
    part_sems,
    text_back_sems,
    vis_back_sems,
):
    me = lax.axis_index("dp")
    core = lax.axis_index("tensor")
    other = 1 - core
    rows = text_buf.shape[1]
    text_half = rows // 2
    cols = text_buf.shape[2]
    width = llm_gain.shape[1]
    sibling = {"tensor": other}
    kv = llm_k_hbm.shape[1]

    def ahead(step):
        return lax.rem(me + step, n)

    def behind(step):
        return lax.rem(me + n - step, n)

    mine = pl.ds(pl.multiple_of(core * text_half, text_half), text_half)
    theirs = pl.ds(pl.multiple_of(other * text_half, text_half), text_half)
    loads = [
        pltpu.make_async_copy(source, target, load_sem.at[i])
        for i, (source, target) in enumerate(
            [
                (text_hbm.at[mine], text),
                (vit_q_hbm, wq),
                (vit_k_hbm, wk),
                (vit_v_hbm, wv),
                (vit_out_hbm, wo),
                (llm_k_hbm, pair_weight.at[:, 0:kv]),
                (llm_v_hbm, pair_weight.at[:, kv : 2 * kv]),
                (merger_hbm, merger),
            ]
        )
    ]
    for load in loads:
        load.start()

    barrier = pltpu.get_barrier_semaphore()

    def greet(step, carry):
        pl.semaphore_signal(barrier, inc=1, device_id={"dp": ahead(step)}, device_id_type=MESH)
        return carry

    lax.fori_loop(1, n, greet, 0)
    pl.semaphore_signal(barrier, inc=1, device_id=sibling, device_id_type=MESH)

    def remote(source, target, send, recv, device):
        return pltpu.make_async_remote_copy(
            src_ref=source,
            dst_ref=target,
            send_sem=send,
            recv_sem=recv,
            device_id=device,
            device_id_type=MESH,
        )

    def text_copy(step):
        start = pl.multiple_of(ahead(step) * cols, cols)
        return remote(
            text_in.at[:, pl.ds(start, cols)],
            text_buf.at[step, mine],
            text_sems.at[0, step],
            text_sems.at[1, step],
            {"dp": ahead(step)},
        )

    def forward_copy(step):
        return remote(
            text_buf.at[step, mine],
            text_buf.at[step, mine],
            forward_sems.at[0, step],
            forward_sems.at[1, step],
            sibling,
        )

    def merged_copy(step):
        return remote(
            merged.at[0],
            merged.at[step],
            merged_sems.at[0, step],
            merged_sems.at[1, step],
            {"dp": ahead(step)},
        )

    def text_back(step):
        return remote(
            text_send.at[step],
            text_recv.at[step],
            text_back_sems.at[0, step],
            text_back_sems.at[1, step],
            {"dp": behind(step)},
        )

    def vis_back(step):
        return remote(
            vis_send.at[step],
            vis_recv.at[step],
            vis_back_sems.at[0, step],
            vis_back_sems.at[1, step],
            {"dp": ahead(step)},
        )

    def each(first, act):
        def run(step, carry):
            act(step)
            return carry

        lax.fori_loop(first, n, run, 0)

    loads[0].wait()

    def norm_rows(i, carry):
        at = pl.ds(pl.multiple_of(i * 16, 16), 16)
        text_in[at, :] = rms_norm(text[at, :], llm_gain[...]).astype(jnp.bfloat16)
        return carry

    lax.fori_loop(0, text_half // 16, norm_rows, 0)
    own_cols = pl.ds(pl.multiple_of(me * cols, cols), cols)
    text_buf[0, mine, :] = text_in[:, own_cols]
    pl.semaphore_wait(barrier, n)
    each(1, lambda step: text_copy(step).start())
    forward_copy(0).start()

    normed = layer_norm(patches[...], vit_gain[...]).astype(jnp.bfloat16)
    for load, weight, place in zip(loads[1:4], (wq, wk, wv), (query, keys, values)):
        load.wait()
        place[...] = dot32(normed, weight[...]).astype(jnp.bfloat16)
    same = image_col[...] == image_row[...]
    mixed[...] = jnp.zeros_like(mixed)
    for head in range(query.shape[1] // VHD):
        low = head * VHD
        base = low // 128 * 128
        end = -(-(low + VHD) // 128) * 128
        lane = lax.broadcasted_iota(jnp.int32, (query.shape[0], end - base), 1)
        inside = (lane >= low - base) & (lane < low - base + VHD)
        q = jnp.where(inside, query[:, base:end].astype(jnp.float32), 0.0).astype(jnp.bfloat16)
        v = jnp.where(inside, values[:, base:end].astype(jnp.float32), 0.0).astype(jnp.bfloat16)
        scores = lax.dot_general(
            q, keys[:, base:end], (((1,), (1,)), ((), ())), preferred_element_type=jnp.float32
        ) * (1.0 / math.sqrt(VHD))
        scores = jnp.where(same, scores, NEG_LARGE)
        scores = jnp.exp(scores - jnp.max(scores, axis=1, keepdims=True))
        weights = (scores / jnp.sum(scores, axis=1, keepdims=True)).astype(jnp.bfloat16)
        mixed[:, base:end] += dot32(weights, v)
    loads[4].wait()
    mix[...] = dot32(mixed[...].astype(jnp.bfloat16), wo[...])
    half = mix.shape[0] // 2
    own_half = pl.ds(pl.multiple_of(core * half, half), half)
    other_half = pl.ds(pl.multiple_of(other * half, half), half)
    swap = remote(mix.at[other_half], mix_recv, mix_sems.at[0], mix_sems.at[1], sibling)
    swap.start()
    swap.wait()
    hidden = (patches[own_half, :].astype(jnp.float32) + (mix[own_half, :] + mix_recv[...])).astype(
        jnp.bfloat16
    )
    normal = layer_norm(hidden, merge_gain[...]).astype(jnp.bfloat16)
    vision_width = normal.shape[1]
    merged[0, :, 0:vision_width] = normal[: half // 2]
    merged[0, :, vision_width : 2 * vision_width] = normal[half // 2 :]
    each(1, lambda step: merged_copy(step).start())

    def hand_over(step):
        text_copy(step).wait_recv()
        forward_copy(step).start()

    each(1, hand_over)
    loads[5].wait()
    loads[6].wait()

    def project_text(step):
        forward_copy(step).wait_recv()
        text_send[step] = dot32(text_buf[step], pair_weight[...]).astype(jnp.bfloat16)

    project_text(0)

    def project_and_send(step):
        project_text(step)
        text_back(step).start()

    each(1, project_and_send)

    loads[7].wait()
    each(1, lambda step: merged_copy(step).wait_recv())
    gathered = merged[...].reshape(-1, merged.shape[2])
    block = 256

    def part_copy(i):
        at = pl.ds(pl.multiple_of(i * block, block), block)
        return remote(
            part.at[:, at], part_recv.at[:, at], part_sems.at[0, i], part_sems.at[1, i], sibling
        )

    for i in range(cols // block):
        at = slice(i * block, (i + 1) * block)
        part[:, at] = dot32(gathered, merger[:, at])
        part_copy(i).start()
    tokens = part.shape[0]
    power = jnp.zeros((tokens, 1), jnp.float32)
    pair = jnp.zeros((tokens, 2 * kv), jnp.float32)
    for i in range(cols // block):
        at = slice(i * block, (i + 1) * block)
        part_copy(i).wait_recv()
        wide = (part[:, at] + part_recv[:, at]).astype(jnp.bfloat16).astype(jnp.float32)
        power = power + jnp.sum(wide * wide, axis=1, keepdims=True)
        gain = llm_gain[:, pl.ds(pl.multiple_of(me * cols + i * block, block), block)]
        pair = pair + dot32((wide * gain).astype(jnp.bfloat16), pair_weight[at, :])
    coarse = power.astype(jnp.bfloat16).astype(jnp.float32)
    lane = lax.broadcasted_iota(jnp.int32, (tokens, MARK), 1)
    marks = jnp.where(lane < MARK // 2, coarse, power - coarse)
    row = jnp.concatenate([pair.astype(jnp.bfloat16), marks.astype(jnp.bfloat16)], axis=1)

    def route(step):
        vis_send[step] = dot32(selector[step], row).astype(jnp.bfloat16)

    route(0)

    def route_and_send(step):
        route(step)
        vis_back(step).start()

    each(1, route_and_send)

    slots = vis_send.shape[1]

    def add_text(step, total):
        text_back(step).wait_recv()
        return total + text_recv[step].astype(jnp.float32)

    out[slots:, :] = lax.fori_loop(1, n, add_text, text_send[0].astype(jnp.float32)).astype(
        jnp.bfloat16
    )

    def add_visual(step, total):
        vis_back(step).wait_recv()
        return total + vis_recv[step].astype(jnp.float32)

    total = lax.fori_loop(1, n, add_visual, vis_send[0].astype(jnp.float32))
    squares = jnp.sum(total[:, 2 * kv :], axis=1, keepdims=True) * (2.0 / MARK)
    out[:slots, :] = (total[:, : 2 * kv] * lax.rsqrt(squares / width + EPSILON)).astype(jnp.bfloat16)

    each(0, lambda step: forward_copy(step).wait_send())
    for i in range(cols // block):
        part_copy(i).wait_send()

    def drain(step):
        text_copy(step).wait_send()
        merged_copy(step).wait_send()
        text_back(step).wait_send()
        vis_back(step).wait_send()

    each(1, drain)


def body(
    patches,
    image_tokens,
    vit_gain,
    vit_q,
    vit_k,
    vit_v,
    vit_out,
    merge_gain,
    merger_out,
    text_rows,
    text_query,
    text_seg,
    vis_route,
    vis_seq,
    llm_gain,
    llm_k,
    llm_v,
):
    devices = lax.axis_size("dp")
    dp_index = lax.axis_index("dp")
    total, width = patches.shape
    ordered = patches.reshape(total // 4, 4, width).transpose(1, 0, 2).reshape(total, width)
    image_of = image_index(image_tokens[0], total).reshape(total // 4, 4).T.reshape(total)
    key_cols = llm_k.shape[1]
    owner_of = vis_route[:, 0]
    token_count = owner_of.shape[0]
    per_block = token_count // devices
    capacity = 2 * per_block // devices
    owner_slots = devices * capacity
    ids = jnp.arange(devices, dtype=jnp.int32)
    owners = owner_of.reshape(devices, per_block)
    earlier = jnp.arange(per_block)[None, :] < jnp.arange(per_block)[:, None]
    alike = (owners[:, :, None] == owners[:, None, :]) & earlier[None]
    rank = jnp.sum(alike.astype(jnp.int32), axis=2)
    local_slot = ids[:, None] * capacity + rank
    slot_ids = jnp.arange(owner_slots, dtype=jnp.int32)
    hits = (owner_of == dp_index)[None, :] & (slot_ids[:, None] == local_slot.reshape(-1)[None, :])
    visual_marker = jnp.sum(jnp.where(hits, (vis_seq + 1)[None, :], 0), axis=1)
    source = (dp_index - ids) % devices
    turned_owner = jnp.sum(
        jnp.where(source[:, None, None] == ids[None, :, None], owners[None], 0), axis=1
    ).reshape(-1)
    turned_slot = jnp.sum(
        jnp.where(source[:, None, None] == ids[None, :, None], local_slot[None], 0), axis=1
    ).reshape(-1)
    target = (dp_index + ids) % devices
    selector = (
        (turned_owner[None, None, :] == target[:, None, None])
        & (turned_slot[None, None, :] == slot_ids[None, :, None])
    ).astype(jnp.bfloat16)

    text_count, model_width = text_rows.shape
    cols = merger_out.shape[1]
    half = total // 2
    vmem = pl.BlockSpec(memory_space=pltpu.VMEM)
    hbm = pl.BlockSpec(memory_space=pl.ANY)
    bf16, f32 = jnp.bfloat16, jnp.float32
    dma = pltpu.SemaphoreType.DMA
    pair = pl.pallas_call(
        functools.partial(kernel, devices),
        out_shape=jax.ShapeDtypeStruct((owner_slots + text_count, 2 * key_cols), bf16),
        in_specs=[vmem] * 4 + [hbm] * 4 + [vmem, hbm, hbm, vmem, vmem, hbm, hbm],
        out_specs=vmem,
        scratch_shapes=[
            pltpu.VMEM(vit_q.shape, bf16),
            pltpu.VMEM(vit_k.shape, bf16),
            pltpu.VMEM(vit_v.shape, bf16),
            pltpu.VMEM(vit_out.shape, bf16),
            pltpu.VMEM(merger_out.shape, bf16),
            pltpu.VMEM((cols, 2 * key_cols), bf16),
            pltpu.VMEM((text_count // 2, model_width), bf16),
            pltpu.VMEM((text_count // 2, model_width), bf16),
            pltpu.VMEM((devices, text_count, cols), bf16),
            pltpu.VMEM((total, vit_q.shape[1]), bf16),
            pltpu.VMEM((total, vit_q.shape[1]), bf16),
            pltpu.VMEM((total, vit_q.shape[1]), bf16),
            pltpu.VMEM((total, vit_q.shape[1]), f32),
            pltpu.VMEM((total, width), f32),
            pltpu.VMEM((half, width), f32),
            pltpu.VMEM((devices, half // 2, 2 * width), bf16),
            pltpu.VMEM((token_count, cols), f32),
            pltpu.VMEM((token_count, cols), f32),
            pltpu.VMEM((devices, text_count, 2 * key_cols), bf16),
            pltpu.VMEM((devices, text_count, 2 * key_cols), bf16),
            pltpu.VMEM((devices, owner_slots, 2 * key_cols + MARK), bf16),
            pltpu.VMEM((devices, owner_slots, 2 * key_cols + MARK), bf16),
            dma((8,)),
            dma((2, devices)),
            dma((2, devices)),
            dma((2,)),
            dma((2, devices)),
            dma((2, cols // 256)),
            dma((2, devices)),
            dma((2, devices)),
        ],
        compiler_params=pltpu.CompilerParams(
            collective_id=0, has_side_effects=True, vmem_limit_bytes=56 * 1024 * 1024
        ),
    )(
        ordered,
        image_of[:, None],
        image_of[None, :],
        vit_gain[None],
        vit_q,
        vit_k,
        vit_v,
        vit_out,
        merge_gain[None],
        merger_out,
        text_rows,
        selector,
        llm_gain[None],
        llm_k,
        llm_v,
    )
    segment = text_seg[0]
    positions = jnp.arange(text_count, dtype=jnp.int32)
    text_allowed = (segment[:, None] == segment[None, :]) & (
        positions[None, :] <= positions[:, None]
    )
    visual_allowed = visual_marker[None, :] == (segment + 1)[:, None]
    allowed = jnp.concatenate([visual_allowed, text_allowed], axis=1)
    local_groups = key_cols // HD
    query_heads = text_query.reshape(text_count, local_groups, QH // KVH, HD)
    all_keys = pair[:, :key_cols].reshape(-1, local_groups, HD)
    all_values = pair[:, key_cols:].reshape(-1, local_groups, HD)
    return local_attention(query_heads, all_keys, all_values, allowed, 1.0 / math.sqrt(HD))


def solution(mesh):
    in_specs = (
        P(("groups", "dp"), None),
        P(("groups", "dp"), None),
        P(),
        P(None, "tensor"),
        P(None, "tensor"),
        P(None, "tensor"),
        P("tensor", None),
        P(),
        P("tensor", "dp"),
        P(("groups", "dp"), None),
        P(("groups", "dp"), "tensor"),
        P(("groups", "dp"), None),
        P("groups", None),
        P("groups"),
        P(),
        P("dp", "tensor"),
        P("dp", "tensor"),
    )
    out_specs = P(("groups", "dp"), "tensor")
    return jax.shard_map(body, mesh=mesh, in_specs=in_specs, out_specs=out_specs, check_vma=False)
```

```python
import functools
import math

import jax
import jax.numpy as jnp
from jax import lax
from jax.experimental import pallas as pl
from jax.experimental.pallas import tpu as pltpu
from jax.sharding import PartitionSpec as P

VHD = 80
QH = 32
KVH = 4
HD = 128


EPSILON = 1e-06
NEG_LARGE = -1e30


def layer_norm(values, scale_gain):
    values = values.astype(jnp.float32)
    centred = values - jnp.mean(values, axis=-1, keepdims=True)
    spread = jnp.mean(centred * centred, axis=-1, keepdims=True)
    return centred * lax.rsqrt(spread + EPSILON) * scale_gain


def rms_norm(values, scale_gain):
    values = values.astype(jnp.float32)
    power = jnp.mean(values * values, axis=-1, keepdims=True)
    return values * lax.rsqrt(power + EPSILON) * scale_gain


def local_attention(query, keys, values, allowed, scale):
    scores = jnp.einsum("tagd,kad->agtk", query, keys, preferred_element_type=jnp.float32) * scale
    scores = jnp.where(allowed[None, None], scores, NEG_LARGE)
    weights = jax.nn.softmax(scores, axis=-1).astype(jnp.bfloat16)
    mixed = jnp.einsum("agtk,kad->tagd", weights, values, preferred_element_type=jnp.float32)
    return mixed.reshape(query.shape[0], -1).astype(jnp.bfloat16)


MESH = pl.DeviceIdType.MESH
MARK = 128


def dot32(left, right):
    return jnp.dot(left, right, preferred_element_type=jnp.float32)


def kernel(
    n,
    patches,
    image_tokens,
    vit_gain,
    vit_q_hbm,
    vit_k_hbm,
    vit_v_hbm,
    vit_out_hbm,
    merge_gain,
    merger_hbm,
    text_hbm,
    route,
    vis_seq,
    llm_gain_flat,
    llm_k_hbm,
    llm_v_hbm,
    out,
    marker,
    code,
    llm_gain,
    ordered,
    wq,
    wk,
    wv,
    wo,
    merger,
    pair_weight,
    text,
    text_in,
    text_buf,
    query,
    keys,
    values,
    mixed,
    mix,
    mix_recv,
    merged,
    part,
    part_recv,
    text_send,
    text_recv,
    vis_send,
    vis_recv,
    load_sem,
    text_sems,
    forward_sems,
    mix_sems,
    merged_sems,
    part_sems,
    text_back_sems,
    vis_back_sems,
    weight_sems,
    twin_sems,
):
    me = lax.axis_index("dp")
    core = lax.axis_index("tensor")
    other = 1 - core
    rows = text_buf.shape[1]
    text_half = rows // 2
    cols = merger.shape[1]
    width = llm_gain.shape[1]
    nz = n // 2
    z, y = me // 2, lax.rem(me, 2)
    mate = {"dp": me + 1 - 2 * y}
    sibling = {"tensor": other}
    kv = llm_k_hbm.shape[1]

    def ahead(step):
        return lax.rem(me + step, n)

    def z_ahead(step):
        return lax.rem(z + step, nz)

    def z_behind(step):
        return lax.rem(z + nz - step, nz)

    mine = pl.ds(pl.multiple_of(core * text_half, text_half), text_half)
    theirs = pl.ds(pl.multiple_of(other * text_half, text_half), text_half)
    own_weight = pl.ds(pl.multiple_of(y * cols, cols), cols)
    loads = [
        pltpu.make_async_copy(source, target, load_sem.at[i])
        for i, (source, target) in enumerate(
            [
                (text_hbm.at[mine], text),
                (vit_q_hbm, wq),
                (vit_k_hbm, wk),
                (vit_v_hbm, wv),
                (vit_out_hbm, wo),
                (llm_k_hbm, pair_weight.at[own_weight, 0:kv]),
                (llm_v_hbm, pair_weight.at[own_weight, kv : 2 * kv]),
                (merger_hbm, merger),
            ]
        )
    ]
    for load in loads:
        load.start()

    barrier = pltpu.get_barrier_semaphore()

    def greet(step, carry):
        pl.semaphore_signal(barrier, inc=1, device_id={"dp": ahead(step)}, device_id_type=MESH)
        return carry

    lax.fori_loop(1, n, greet, 0)
    pl.semaphore_signal(barrier, inc=1, device_id=sibling, device_id_type=MESH)

    def remote(source, target, send, recv, device):
        return pltpu.make_async_remote_copy(
            src_ref=source,
            dst_ref=target,
            send_sem=send,
            recv_sem=recv,
            device_id=device,
            device_id_type=MESH,
        )

    def text_copy(step):
        start = pl.multiple_of(z_ahead(step) * 2 * cols, 2 * cols)
        return remote(
            text_in.at[:, pl.ds(start, 2 * cols)],
            text_buf.at[step, mine],
            text_sems.at[0, step],
            text_sems.at[1, step],
            {"dp": z_ahead(step) * 2 + y},
        )

    def forward_copy(step):
        return remote(
            text_buf.at[step, mine],
            text_buf.at[step, mine],
            forward_sems.at[0, step],
            forward_sems.at[1, step],
            sibling,
        )

    def merged_copy(step):
        return remote(
            merged.at[0],
            merged.at[2 * step],
            merged_sems.at[0, step],
            merged_sems.at[1, step],
            {"dp": z_ahead(step) * 2 + y},
        )

    def twin_copy(step):
        return remote(
            merged.at[2 * step],
            merged.at[2 * step + 1],
            twin_sems.at[0, step],
            twin_sems.at[1, step],
            mate,
        )

    def weight_copy():
        return remote(
            pair_weight.at[own_weight],
            pair_weight.at[own_weight],
            weight_sems.at[0],
            weight_sems.at[1],
            mate,
        )

    def text_back(step):
        return remote(
            text_send.at[step],
            text_recv.at[step],
            text_back_sems.at[0, step],
            text_back_sems.at[1, step],
            {"dp": z_behind(step) * 2 + y},
        )

    def vis_back(step):
        return remote(
            vis_send.at[step],
            vis_recv.at[step],
            vis_back_sems.at[0, step],
            vis_back_sems.at[1, step],
            {"dp": ahead(step)},
        )

    def each(first, last, act):
        def run(step, carry):
            act(step)
            return carry

        lax.fori_loop(first, last, run, 0)

    llm_gain[...] = llm_gain_flat[...].reshape(1, -1)

    loads[0].wait()

    def norm_rows(i, carry):
        at = pl.ds(pl.multiple_of(i * 16, 16), 16)
        text_in[at, :] = rms_norm(text[at, :], llm_gain[...]).astype(jnp.bfloat16)
        return carry

    lax.fori_loop(0, text_half // 16, norm_rows, 0)
    own_cols = pl.ds(pl.multiple_of(z * 2 * cols, 2 * cols), 2 * cols)
    text_buf[0, mine, :] = text_in[:, own_cols]
    pl.semaphore_wait(barrier, n)
    each(1, nz, lambda step: text_copy(step).start())
    forward_copy(0).start()
    loads[5].wait()
    loads[6].wait()
    weight_copy().start()

    count = patches.shape[0]
    quarter = count // 4

    def token_of(place):
        part_of = sum([(place >= j * quarter).astype(jnp.int32) for j in range(1, 4)])
        return place - quarter * part_of, part_of

    def image_at(place):
        token, end, image = token_of(place)[0], 0, 0
        for i in range(image_tokens.shape[1]):
            end = end + image_tokens[0, i]
            image = image + (token >= end).astype(jnp.int32)
        return image

    down = lax.broadcasted_iota(jnp.int32, (count, count), 0)
    across = lax.broadcasted_iota(jnp.int32, (count, count), 1)
    token, place = token_of(down)
    chosen = jnp.where(across == 4 * token + place, 1.0, 0.0).astype(jnp.bfloat16)
    ordered[...] = dot32(chosen, patches[...])

    normed = layer_norm(ordered[...], vit_gain[...].reshape(1, -1)).astype(jnp.bfloat16)
    for load, weight, place in zip(loads[1:4], (wq, wk, wv), (query, keys, values)):
        load.wait()
        place[...] = dot32(normed, weight[...]).astype(jnp.bfloat16)
    same = image_at(down) == image_at(across)
    mixed[...] = jnp.zeros_like(mixed)
    for head in range(query.shape[1] // VHD):
        low = head * VHD
        base = low // 128 * 128
        end = -(-(low + VHD) // 128) * 128
        lane = lax.broadcasted_iota(jnp.int32, (query.shape[0], end - base), 1)
        inside = (lane >= low - base) & (lane < low - base + VHD)
        q = jnp.where(inside, query[:, base:end].astype(jnp.float32), 0.0).astype(jnp.bfloat16)
        v = jnp.where(inside, values[:, base:end].astype(jnp.float32), 0.0).astype(jnp.bfloat16)
        scores = lax.dot_general(
            q, keys[:, base:end], (((1,), (1,)), ((), ())), preferred_element_type=jnp.float32
        ) * (1.0 / math.sqrt(VHD))
        scores = jnp.where(same, scores, NEG_LARGE)
        scores = jnp.exp(scores - jnp.max(scores, axis=1, keepdims=True))
        weights = (scores / jnp.sum(scores, axis=1, keepdims=True)).astype(jnp.bfloat16)
        mixed[:, base:end] += dot32(weights, v)
    loads[4].wait()
    mix[...] = dot32(mixed[...].astype(jnp.bfloat16), wo[...])
    half = mix.shape[0] // 2
    own_half = pl.ds(pl.multiple_of(core * half, half), half)
    other_half = pl.ds(pl.multiple_of(other * half, half), half)
    swap = remote(mix.at[other_half], mix_recv, mix_sems.at[0], mix_sems.at[1], sibling)
    swap.start()
    swap.wait()
    hidden = (ordered[own_half, :] + (mix[own_half, :] + mix_recv[...])).astype(
        jnp.bfloat16
    )
    normal = layer_norm(hidden, merge_gain[...].reshape(1, -1)).astype(jnp.bfloat16)
    vision_width = normal.shape[1]
    merged[0, :, 0:vision_width] = normal[: half // 2]
    merged[0, :, vision_width : 2 * vision_width] = normal[half // 2 :]
    each(1, nz, lambda step: merged_copy(step).start())
    twin_copy(0).start()

    slots = vis_send.shape[1]
    per_block = code.shape[0] // n
    capacity = slots // n
    lanes = lax.broadcasted_iota(jnp.int32, (per_block, 128), 1)
    before = jnp.where(
        lax.broadcasted_iota(jnp.int32, (per_block, per_block), 1)
        < lax.broadcasted_iota(jnp.int32, (per_block, per_block), 0),
        1.0,
        0.0,
    ).astype(jnp.bfloat16)
    slot_of = lax.broadcasted_iota(jnp.int32, (per_block, slots), 1) + me * slots

    def place_block(i, total):
        parity = lax.rem(i, 2)
        source = z_behind(i // 2) * 2 + lax.rem(y + parity, 2)
        at = pl.ds(pl.multiple_of(source * per_block, per_block), per_block)
        owner = route[at, :]
        onehot = jnp.where(lanes == owner, 1.0, 0.0)
        earlier = dot32(before, onehot.astype(jnp.bfloat16))
        rank = jnp.sum(earlier * onehot, axis=1, keepdims=True).astype(jnp.int32)
        number = owner * slots + source * capacity + rank
        code[pl.ds(pl.multiple_of(i * per_block, per_block), per_block), :] = number
        named = jnp.where(number == slot_of, vis_seq[at, :] + 1, 0)
        return total + jnp.sum(named, axis=0, keepdims=True)

    marker[...] = lax.fori_loop(0, n, place_block, jnp.zeros((1, slots), jnp.int32))

    def hand_over(step):
        text_copy(step).wait_recv()
        forward_copy(step).start()

    each(1, nz, hand_over)

    def pass_on(step):
        merged_copy(step).wait_recv()
        twin_copy(step).start()

    each(1, nz, pass_on)
    weight_copy().wait_recv()

    def project_text(step):
        forward_copy(step).wait_recv()
        text_send[step] = dot32(text_buf[step], pair_weight[...]).astype(jnp.bfloat16)

    def project_and_send(step):
        project_text(step)
        text_back(step).start()

    each(1, nz, project_and_send)
    project_text(0)

    loads[7].wait()
    each(0, nz, lambda step: twin_copy(step).wait_recv())
    gathered = merged[...].reshape(-1, merged.shape[2])
    block = 256

    def part_copy(i):
        at = pl.ds(pl.multiple_of(i * block, block), block)
        return remote(
            part.at[:, at], part_recv.at[:, at], part_sems.at[0, i], part_sems.at[1, i], sibling
        )

    for i in range(cols // block):
        at = slice(i * block, (i + 1) * block)
        part[:, at] = dot32(gathered, merger[:, at])
        part_copy(i).start()
    tokens = part.shape[0]
    power = jnp.zeros((tokens, 1), jnp.float32)
    pair = jnp.zeros((tokens, 2 * kv), jnp.float32)
    for i in range(cols // block):
        at = slice(i * block, (i + 1) * block)
        part_copy(i).wait_recv()
        wide = (part[:, at] + part_recv[:, at]).astype(jnp.bfloat16).astype(jnp.float32)
        power = power + jnp.sum(wide * wide, axis=1, keepdims=True)
        gain = llm_gain[:, pl.ds(pl.multiple_of(me * cols + i * block, block), block)]
        weight = pair_weight[pl.ds(pl.multiple_of(y * cols + i * block, block), block), :]
        pair = pair + dot32((wide * gain).astype(jnp.bfloat16), weight)
    coarse = power.astype(jnp.bfloat16).astype(jnp.float32)
    lane = lax.broadcasted_iota(jnp.int32, (tokens, MARK), 1)
    marks = jnp.where(lane < MARK // 2, coarse, power - coarse)
    row = jnp.concatenate([pair.astype(jnp.bfloat16), marks.astype(jnp.bfloat16)], axis=1)

    def route_to(step):
        wanted = lax.broadcasted_iota(jnp.int32, (tokens, slots), 1) + ahead(step) * slots
        picked = jnp.where(code[...] == wanted, 1.0, 0.0).astype(jnp.bfloat16)
        vis_send[step] = lax.dot_general(
            picked, row, (((0,), (0,)), ((), ())), preferred_element_type=jnp.float32
        ).astype(jnp.bfloat16)

    route_to(0)

    def route_and_send(step):
        route_to(step)
        vis_back(step).start()

    each(1, n, route_and_send)


    def add_text(step, total):
        text_back(step).wait_recv()
        return total + text_recv[step].astype(jnp.float32)

    out[slots:, :] = lax.fori_loop(1, nz, add_text, text_send[0].astype(jnp.float32)).astype(
        jnp.bfloat16
    )

    def add_visual(step, total):
        vis_back(step).wait_recv()
        return total + vis_recv[step].astype(jnp.float32)

    total = lax.fori_loop(1, n, add_visual, vis_send[0].astype(jnp.float32))
    squares = jnp.sum(total[:, 2 * kv :], axis=1, keepdims=True) * (2.0 / MARK)
    out[:slots, :] = (total[:, : 2 * kv] * lax.rsqrt(squares / width + EPSILON)).astype(jnp.bfloat16)

    each(0, nz, lambda step: forward_copy(step).wait_send())
    each(0, nz, lambda step: twin_copy(step).wait_send())
    weight_copy().wait_send()
    for i in range(cols // block):
        part_copy(i).wait_send()

    def drain(step):
        text_copy(step).wait_send()
        merged_copy(step).wait_send()
        text_back(step).wait_send()

    each(1, nz, drain)
    each(1, n, lambda step: vis_back(step).wait_send())


def body(
    patches,
    image_tokens,
    vit_gain,
    vit_q,
    vit_k,
    vit_v,
    vit_out,
    merge_gain,
    merger_out,
    text_rows,
    text_query,
    text_seg,
    vis_route,
    vis_seq,
    llm_gain,
    llm_k,
    llm_v,
):
    devices = lax.axis_size("dp")
    total, width = patches.shape
    key_cols = llm_k.shape[1]
    token_count = vis_route.shape[0]
    owner_slots = 2 * token_count // devices
    text_count, model_width = text_rows.shape
    cols = merger_out.shape[1]
    half = total // 2
    vmem = pl.BlockSpec(memory_space=pltpu.VMEM)
    smem = pl.BlockSpec(memory_space=pltpu.SMEM)
    hbm = pl.BlockSpec(memory_space=pl.ANY)
    bf16, f32 = jnp.bfloat16, jnp.float32
    dma = pltpu.SemaphoreType.DMA
    pairs = devices // 2
    pair, visual_marker = pl.pallas_call(
        functools.partial(kernel, devices),
        out_shape=(
            jax.ShapeDtypeStruct((owner_slots + text_count, 2 * key_cols), bf16),
            jax.ShapeDtypeStruct((1, owner_slots), jnp.int32),
        ),
        in_specs=[vmem, smem, vmem] + [hbm] * 4 + [vmem, hbm, hbm, vmem, vmem, vmem, hbm, hbm],
        out_specs=(vmem, vmem),
        scratch_shapes=[
            pltpu.VMEM((token_count, 1), jnp.int32),
            pltpu.VMEM((1, model_width), f32),
            pltpu.VMEM((total, width), f32),
            pltpu.VMEM(vit_q.shape, bf16),
            pltpu.VMEM(vit_k.shape, bf16),
            pltpu.VMEM(vit_v.shape, bf16),
            pltpu.VMEM(vit_out.shape, bf16),
            pltpu.VMEM(merger_out.shape, bf16),
            pltpu.VMEM((2 * cols, 2 * key_cols), bf16),
            pltpu.VMEM((text_count // 2, model_width), bf16),
            pltpu.VMEM((text_count // 2, model_width), bf16),
            pltpu.VMEM((pairs, text_count, 2 * cols), bf16),
            pltpu.VMEM((total, vit_q.shape[1]), bf16),
            pltpu.VMEM((total, vit_q.shape[1]), bf16),
            pltpu.VMEM((total, vit_q.shape[1]), bf16),
            pltpu.VMEM((total, vit_q.shape[1]), f32),
            pltpu.VMEM((total, width), f32),
            pltpu.VMEM((half, width), f32),
            pltpu.VMEM((devices, half // 2, 2 * width), bf16),
            pltpu.VMEM((token_count, cols), f32),
            pltpu.VMEM((token_count, cols), f32),
            pltpu.VMEM((pairs, text_count, 2 * key_cols), bf16),
            pltpu.VMEM((pairs, text_count, 2 * key_cols), bf16),
            pltpu.VMEM((devices, owner_slots, 2 * key_cols + MARK), bf16),
            pltpu.VMEM((devices, owner_slots, 2 * key_cols + MARK), bf16),
            dma((8,)),
            dma((2, devices)),
            dma((2, devices)),
            dma((2,)),
            dma((2, devices)),
            dma((2, cols // 256)),
            dma((2, devices)),
            dma((2, devices)),
            dma((2,)),
            dma((2, pairs)),
        ],
        compiler_params=pltpu.CompilerParams(
            collective_id=0, has_side_effects=True, vmem_limit_bytes=56 * 1024 * 1024
        ),
    )(
        patches,
        image_tokens,
        vit_gain,
        vit_q,
        vit_k,
        vit_v,
        vit_out,
        merge_gain,
        merger_out,
        text_rows,
        vis_route,
        vis_seq[:, None],
        llm_gain,
        llm_k,
        llm_v,
    )
    segment = text_seg[0]
    positions = jnp.arange(text_count, dtype=jnp.int32)
    text_allowed = (segment[:, None] == segment[None, :]) & (
        positions[None, :] <= positions[:, None]
    )
    visual_allowed = visual_marker == (segment + 1)[:, None]
    allowed = jnp.concatenate([visual_allowed, text_allowed], axis=1)
    local_groups = key_cols // HD
    query_heads = text_query.reshape(text_count, local_groups, QH // KVH, HD)
    all_keys = pair[:, :key_cols].reshape(-1, local_groups, HD)
    all_values = pair[:, key_cols:].reshape(-1, local_groups, HD)
    return local_attention(query_heads, all_keys, all_values, allowed, 1.0 / math.sqrt(HD))


def solution(mesh):
    in_specs = (
        P(("groups", "dp"), None),
        P(("groups", "dp"), None),
        P(),
        P(None, "tensor"),
        P(None, "tensor"),
        P(None, "tensor"),
        P("tensor", None),
        P(),
        P("tensor", "dp"),
        P(("groups", "dp"), None),
        P(("groups", "dp"), "tensor"),
        P(("groups", "dp"), None),
        P("groups", None),
        P("groups"),
        P(),
        P("dp", "tensor"),
        P("dp", "tensor"),
    )
    out_specs = P(("groups", "dp"), "tensor")
    return jax.shard_map(body, mesh=mesh, in_specs=in_specs, out_specs=out_specs, check_vma=False)
```

```python
import functools
import math

import jax
import jax.numpy as jnp
from jax import lax
from jax.experimental import pallas as pl
from jax.experimental.pallas import tpu as pltpu
from jax.sharding import PartitionSpec as P

VHD = 80
QH = 32
KVH = 4
HD = 128


EPSILON = 1e-06
NEG_LARGE = -1e30


def layer_norm(values, scale_gain):
    values = values.astype(jnp.float32)
    centred = values - jnp.mean(values, axis=-1, keepdims=True)
    spread = jnp.mean(centred * centred, axis=-1, keepdims=True)
    return centred * lax.rsqrt(spread + EPSILON) * scale_gain


def local_attention(query, keys, values, allowed, scale):
    scores = jnp.einsum("tagd,kad->agtk", query, keys, preferred_element_type=jnp.float32) * scale
    scores = jnp.where(allowed[None, None], scores, NEG_LARGE)
    weights = jax.nn.softmax(scores, axis=-1).astype(jnp.bfloat16)
    mixed = jnp.einsum("agtk,kad->tagd", weights, values, preferred_element_type=jnp.float32)
    return mixed.reshape(query.shape[0], -1).astype(jnp.bfloat16)


MESH = pl.DeviceIdType.MESH
MARK = 128


def dot32(left, right):
    return jnp.dot(left, right, preferred_element_type=jnp.float32)


def kernel(
    n,
    patches,
    image_tokens,
    vit_gain,
    vit_q_hbm,
    vit_k_hbm,
    vit_v_hbm,
    vit_out_hbm,
    merge_gain,
    merger_hbm,
    text_hbm,
    route,
    vis_seq,
    llm_gain_flat,
    llm_k_hbm,
    llm_v_hbm,
    out,
    marker,
    code,
    llm_gain,
    ordered,
    wq,
    wk,
    wv,
    wo,
    merger,
    pair_weight,
    text,
    text_scale,
    route_wide,
    seq_wide,
    text_buf,
    query,
    keys,
    values,
    mixed,
    mix,
    mix_recv,
    merged,
    part,
    part_recv,
    text_send,
    text_sum,
    text_recv,
    vis_send,
    vis_recv,
    vis_mate,
    vis_mate_recv,
    vis_sum,
    load_sem,
    text_sems,
    forward_sems,
    mix_sems,
    merged_sems,
    part_sems,
    text_back_sems,
    vis_back_sems,
    weight_sems,
    twin_sems,
    mate_sems,
):
    me = lax.axis_index("dp")
    core = lax.axis_index("tensor")
    other = 1 - core
    rows = text_buf.shape[1]
    text_half = rows // 2
    cols = merger.shape[1]
    width = llm_gain.shape[1]
    nz = n // 2
    z, y = me // 2, lax.rem(me, 2)
    mate = {"dp": me + 1 - 2 * y}
    sibling = {"tensor": other}
    kv = llm_k_hbm.shape[1]

    def z_ahead(step):
        return lax.rem(z + step, nz)

    def z_behind(step):
        return lax.rem(z + nz - step, nz)

    mine = pl.ds(pl.multiple_of(core * text_half, text_half), text_half)
    theirs = pl.ds(pl.multiple_of(other * text_half, text_half), text_half)
    own_weight = pl.ds(pl.multiple_of(y * cols, cols), cols)
    loads = [
        pltpu.make_async_copy(source, target, load_sem.at[i])
        for i, (source, target) in enumerate(
            [
                (text_hbm, text),
                (vit_q_hbm, wq),
                (vit_k_hbm, wk),
                (vit_v_hbm, wv),
                (vit_out_hbm, wo),
                (llm_k_hbm, pair_weight.at[own_weight, 0:kv]),
                (llm_v_hbm, pair_weight.at[own_weight, kv : 2 * kv]),
                (merger_hbm, merger),
            ]
        )
    ]
    for load in loads:
        load.start()

    barrier = pltpu.get_barrier_semaphore()

    def greet(step, carry):
        peer = {"dp": z_ahead(step) * 2 + y}
        pl.semaphore_signal(barrier, inc=1, device_id=peer, device_id_type=MESH)
        return carry

    lax.fori_loop(1, nz, greet, 0)
    pl.semaphore_signal(barrier, inc=1, device_id=mate, device_id_type=MESH)
    pl.semaphore_signal(barrier, inc=1, device_id=sibling, device_id_type=MESH)

    def remote(source, target, send, recv, device):
        return pltpu.make_async_remote_copy(
            src_ref=source,
            dst_ref=target,
            send_sem=send,
            recv_sem=recv,
            device_id=device,
            device_id_type=MESH,
        )

    def text_copy(step):
        start = pl.multiple_of(z_ahead(step) * 2 * cols, 2 * cols)
        return remote(
            text_hbm.at[mine, pl.ds(start, 2 * cols)],
            text_buf.at[step, mine],
            text_sems.at[0, step],
            text_sems.at[1, step],
            {"dp": z_ahead(step) * 2 + y},
        )

    def forward_copy(step):
        return remote(
            text_buf.at[step, mine],
            text_buf.at[step, mine],
            forward_sems.at[0, step],
            forward_sems.at[1, step],
            sibling,
        )

    def merged_copy(step):
        return remote(
            merged.at[0],
            merged.at[2 * step],
            merged_sems.at[0, step],
            merged_sems.at[1, step],
            {"dp": z_ahead(step) * 2 + y},
        )

    def twin_copy(step):
        return remote(
            merged.at[2 * step],
            merged.at[2 * step + 1],
            twin_sems.at[0, step],
            twin_sems.at[1, step],
            mate,
        )

    def weight_copy():
        return remote(
            pair_weight.at[own_weight],
            pair_weight.at[own_weight],
            weight_sems.at[0],
            weight_sems.at[1],
            mate,
        )

    def text_back(step):
        return remote(
            text_send.at[step],
            text_recv.at[step],
            text_back_sems.at[0, step],
            text_back_sems.at[1, step],
            {"dp": z_behind(step) * 2 + y},
        )

    def vis_back(step):
        return remote(
            vis_send.at[step],
            vis_recv.at[step],
            vis_back_sems.at[0, step],
            vis_back_sems.at[1, step],
            {"dp": z_ahead(step) * 2 + y},
        )

    def mate_copy(step):
        return remote(
            vis_mate.at[step],
            vis_mate_recv.at[step],
            mate_sems.at[0, step],
            mate_sems.at[1, step],
            mate,
        )

    def each(first, last, act):
        def run(step, carry):
            act(step)
            return carry

        lax.fori_loop(first, last, run, 0)

    llm_gain[...] = llm_gain_flat[...].reshape(1, -1)

    own_cols = pl.ds(pl.multiple_of(z * 2 * cols, 2 * cols), 2 * cols)
    own_text = pltpu.make_async_copy(text_hbm.at[:, own_cols], text_buf.at[0], load_sem.at[8])
    own_text.start()
    pl.semaphore_wait(barrier, nz + 1)
    each(1, nz, lambda step: text_copy(step).start())
    loads[5].wait()
    loads[6].wait()
    weight_copy().start()

    count = patches.shape[0]
    quarter = count // 4

    def token_of(place):
        part_of = sum([(place >= j * quarter).astype(jnp.int32) for j in range(1, 4)])
        return place - quarter * part_of, part_of

    def image_at(place):
        token, end, image = token_of(place)[0], 0, 0
        for i in range(image_tokens.shape[1]):
            end = end + image_tokens[0, i]
            image = image + (token >= end).astype(jnp.int32)
        return image

    down = lax.broadcasted_iota(jnp.int32, (count, count), 0)
    across = lax.broadcasted_iota(jnp.int32, (count, count), 1)
    token, place = token_of(down)
    chosen = jnp.where(across == 4 * token + place, 1.0, 0.0).astype(jnp.bfloat16)
    ordered[...] = dot32(chosen, patches[...])

    normed = layer_norm(ordered[...], vit_gain[...].reshape(1, -1)).astype(jnp.bfloat16)
    for load, weight, place in zip(loads[1:4], (wq, wk, wv), (query, keys, values)):
        load.wait()
        place[...] = dot32(normed, weight[...]).astype(jnp.bfloat16)
    same = image_at(down) == image_at(across)
    mixed[...] = jnp.zeros_like(mixed)
    for head in range(query.shape[1] // VHD):
        low = head * VHD
        base = low // 128 * 128
        end = -(-(low + VHD) // 128) * 128
        lane = lax.broadcasted_iota(jnp.int32, (query.shape[0], end - base), 1)
        inside = (lane >= low - base) & (lane < low - base + VHD)
        q = jnp.where(inside, query[:, base:end].astype(jnp.float32), 0.0).astype(jnp.bfloat16)
        v = jnp.where(inside, values[:, base:end].astype(jnp.float32), 0.0).astype(jnp.bfloat16)
        scores = lax.dot_general(
            q, keys[:, base:end], (((1,), (1,)), ((), ())), preferred_element_type=jnp.float32
        ) * (1.0 / math.sqrt(VHD))
        scores = jnp.where(same, scores, NEG_LARGE)
        scores = jnp.exp(scores - jnp.max(scores, axis=1, keepdims=True))
        weights = (scores / jnp.sum(scores, axis=1, keepdims=True)).astype(jnp.bfloat16)
        mixed[:, base:end] += dot32(weights, v)
    loads[4].wait()
    mix[...] = dot32(mixed[...].astype(jnp.bfloat16), wo[...])
    half = mix.shape[0] // 2
    own_half = pl.ds(pl.multiple_of(core * half, half), half)
    other_half = pl.ds(pl.multiple_of(other * half, half), half)
    swap = remote(mix.at[other_half], mix_recv, mix_sems.at[0], mix_sems.at[1], sibling)
    swap.start()
    swap.wait()
    hidden = (ordered[own_half, :] + (mix[own_half, :] + mix_recv[...])).astype(
        jnp.bfloat16
    )
    normal = layer_norm(hidden, merge_gain[...].reshape(1, -1)).astype(jnp.bfloat16)
    vision_width = normal.shape[1]
    merged[0, :, 0:vision_width] = normal[: half // 2]
    merged[0, :, vision_width : 2 * vision_width] = normal[half // 2 :]
    each(1, nz, lambda step: merged_copy(step).start())
    twin_copy(0).start()

    route_wide[...] = jnp.broadcast_to(
        route[...].astype(jnp.float32).reshape(1, -1), (128, code.shape[0])
    ).T
    seq_wide[...] = jnp.broadcast_to(
        vis_seq[...].astype(jnp.float32).reshape(1, -1), (128, code.shape[0])
    ).T
    slots = vis_send.shape[1]
    per_block = code.shape[0] // n
    capacity = slots // n
    lanes = lax.broadcasted_iota(jnp.int32, (per_block, 128), 1)
    before = jnp.where(
        lax.broadcasted_iota(jnp.int32, (per_block, per_block), 1)
        < lax.broadcasted_iota(jnp.int32, (per_block, per_block), 0),
        1.0,
        0.0,
    ).astype(jnp.bfloat16)
    slot_of = lax.broadcasted_iota(jnp.int32, (per_block, slots), 1) + me * slots

    def place_block(i, total):
        parity = lax.rem(i, 2)
        source = z_behind(i // 2) * 2 + lax.rem(y + parity, 2)
        at = pl.ds(pl.multiple_of(source * per_block, per_block), per_block)
        owner = route_wide[at, :].astype(jnp.int32)
        onehot = jnp.where(lanes == owner, 1.0, 0.0)
        earlier = dot32(before, onehot.astype(jnp.bfloat16))
        rank = jnp.sum(earlier * onehot, axis=1, keepdims=True).astype(jnp.int32)
        number = owner[:, 0:1] * slots + source * capacity + rank
        code[pl.ds(pl.multiple_of(i * per_block, per_block), per_block), :] = number
        named = jnp.where(number == slot_of, seq_wide[at, 0:slots].astype(jnp.int32) + 1, 0)
        return total + jnp.sum(named, axis=0, keepdims=True)

    marker[...] = lax.fori_loop(0, n, place_block, jnp.zeros((1, slots), jnp.int32))

    def hand_over(step):
        text_copy(step).wait_recv()
        forward_copy(step).start()

    loads[0].wait()

    def scale_rows(i, carry):
        at = pl.ds(pl.multiple_of(i * 16, 16), 16)
        wide = text[at, :].astype(jnp.float32)
        squares = jnp.sum(wide * wide, axis=1, keepdims=True)
        text_scale[at, :] = jnp.broadcast_to(
            lax.rsqrt(squares / width + EPSILON), (16, text_scale.shape[1])
        )
        return carry

    lax.fori_loop(0, rows // 16, scale_rows, 0)
    each(1, nz, hand_over)

    def pass_on(step):
        merged_copy(step).wait_recv()
        twin_copy(step).start()

    each(1, nz, pass_on)
    weight_copy().wait_recv()

    def project_text(step):
        gained = (text_buf[step].astype(jnp.float32) * llm_gain[:, own_cols]).astype(jnp.bfloat16)
        return dot32(gained, pair_weight[...])

    def project_and_send(step):
        forward_copy(step).wait_recv()
        text_send[step] = project_text(step).astype(jnp.bfloat16)
        text_back(step).start()

    each(1, nz, project_and_send)
    own_text.wait()
    text_sum[...] = project_text(0)

    loads[7].wait()
    each(0, nz, lambda step: twin_copy(step).wait_recv())
    gathered = merged[...].reshape(-1, merged.shape[2])
    block = 256

    def part_copy(i):
        at = pl.ds(pl.multiple_of(i * block, block), block)
        return remote(
            part.at[:, at], part_recv.at[:, at], part_sems.at[0, i], part_sems.at[1, i], sibling
        )

    for i in range(cols // block):
        at = slice(i * block, (i + 1) * block)
        part[:, at] = dot32(gathered, merger[:, at])
        part_copy(i).start()
    tokens = part.shape[0]
    power = jnp.zeros((tokens, 1), jnp.float32)
    pair = jnp.zeros((tokens, 2 * kv), jnp.float32)
    for i in range(cols // block):
        at = slice(i * block, (i + 1) * block)
        part_copy(i).wait_recv()
        wide = (part[:, at] + part_recv[:, at]).astype(jnp.bfloat16).astype(jnp.float32)
        power = power + jnp.sum(wide * wide, axis=1, keepdims=True)
        gain = llm_gain[:, pl.ds(pl.multiple_of(me * cols + i * block, block), block)]
        weight = pair_weight[pl.ds(pl.multiple_of(y * cols + i * block, block), block), :]
        pair = pair + dot32((wide * gain).astype(jnp.bfloat16), weight)

    def marked(square):
        coarse = square.astype(jnp.bfloat16).astype(jnp.float32)
        lane = lax.broadcasted_iota(jnp.int32, (square.shape[0], MARK), 1)
        return jnp.where(lane < MARK // 2, coarse, square - coarse).astype(jnp.bfloat16)

    row = jnp.concatenate([pair.astype(jnp.bfloat16), marked(power)], axis=1)

    def route_to(owner):
        wanted = lax.broadcasted_iota(jnp.int32, (tokens, slots), 1) + owner * slots
        picked = jnp.where(code[...] == wanted, 1.0, 0.0).astype(jnp.bfloat16)
        return lax.dot_general(
            picked, row, (((0,), (0,)), ((), ())), preferred_element_type=jnp.float32
        )

    def route_for_mate(step):
        vis_mate[step] = route_to(z_ahead(step) * 2 + 1 - y).astype(jnp.bfloat16)
        mate_copy(step).start()

    def route_own(step):
        total = route_to(z_ahead(step) * 2 + y)
        mate_copy(step).wait_recv()
        return total + vis_mate_recv[step].astype(jnp.float32)

    def route_and_send(step):
        total = route_own(step)
        square = jnp.sum(total[:, 2 * kv :], axis=1, keepdims=True) * (2.0 / MARK)
        vis_send[step, :, 0 : 2 * kv] = total[:, : 2 * kv].astype(jnp.bfloat16)
        vis_send[step, :, 2 * kv :] = marked(square)
        vis_back(step).start()

    each(1, nz, route_for_mate)
    route_for_mate(0)
    each(1, nz, route_and_send)
    vis_sum[...] = route_own(0)


    def add_text(step, total):
        text_back(step).wait_recv()
        return total + text_recv[step].astype(jnp.float32)

    text_total = lax.fori_loop(1, nz, add_text, text_sum[...])
    out[slots:, :] = (text_total * text_scale[:, 0:1]).astype(jnp.bfloat16)

    def add_visual(step, total):
        vis_back(step).wait_recv()
        return total + vis_recv[step].astype(jnp.float32)

    total = lax.fori_loop(1, nz, add_visual, vis_sum[...])
    squares = jnp.sum(total[:, 2 * kv :], axis=1, keepdims=True) * (2.0 / MARK)
    out[:slots, :] = (total[:, : 2 * kv] * lax.rsqrt(squares / width + EPSILON)).astype(jnp.bfloat16)

    each(1, nz, lambda step: forward_copy(step).wait_send())
    each(0, nz, lambda step: twin_copy(step).wait_send())
    weight_copy().wait_send()
    for i in range(cols // block):
        part_copy(i).wait_send()

    def drain(step):
        text_copy(step).wait_send()
        merged_copy(step).wait_send()
        text_back(step).wait_send()

    each(1, nz, drain)
    each(1, nz, lambda step: vis_back(step).wait_send())
    each(0, nz, lambda step: mate_copy(step).wait_send())


def body(
    patches,
    image_tokens,
    vit_gain,
    vit_q,
    vit_k,
    vit_v,
    vit_out,
    merge_gain,
    merger_out,
    text_rows,
    text_query,
    text_seg,
    vis_route,
    vis_seq,
    llm_gain,
    llm_k,
    llm_v,
):
    devices = lax.axis_size("dp")
    total, width = patches.shape
    key_cols = llm_k.shape[1]
    token_count = vis_route.shape[0]
    owner_slots = 2 * token_count // devices
    text_count, model_width = text_rows.shape
    cols = merger_out.shape[1]
    half = total // 2
    vmem = pl.BlockSpec(memory_space=pltpu.VMEM)
    smem = pl.BlockSpec(memory_space=pltpu.SMEM)
    hbm = pl.BlockSpec(memory_space=pl.ANY)
    bf16, f32 = jnp.bfloat16, jnp.float32
    dma = pltpu.SemaphoreType.DMA
    pairs = devices // 2
    pair, visual_marker = pl.pallas_call(
        functools.partial(kernel, devices),
        out_shape=(
            jax.ShapeDtypeStruct((owner_slots + text_count, 2 * key_cols), bf16),
            jax.ShapeDtypeStruct((1, owner_slots), jnp.int32),
        ),
        in_specs=[vmem, smem, vmem] + [hbm] * 4 + [vmem, hbm, hbm, vmem, vmem, vmem, hbm, hbm],
        out_specs=(vmem, vmem),
        scratch_shapes=[
            pltpu.VMEM((token_count, 1), jnp.int32),
            pltpu.VMEM((1, model_width), f32),
            pltpu.VMEM((total, width), f32),
            pltpu.VMEM(vit_q.shape, bf16),
            pltpu.VMEM(vit_k.shape, bf16),
            pltpu.VMEM(vit_v.shape, bf16),
            pltpu.VMEM(vit_out.shape, bf16),
            pltpu.VMEM(merger_out.shape, bf16),
            pltpu.VMEM((2 * cols, 2 * key_cols), bf16),
            pltpu.VMEM((text_count, model_width), bf16),
            pltpu.VMEM((text_count, 128), f32),
            pltpu.VMEM((token_count, 128), f32),
            pltpu.VMEM((token_count, 128), f32),
            pltpu.VMEM((pairs, text_count, 2 * cols), bf16),
            pltpu.VMEM((total, vit_q.shape[1]), bf16),
            pltpu.VMEM((total, vit_q.shape[1]), bf16),
            pltpu.VMEM((total, vit_q.shape[1]), bf16),
            pltpu.VMEM((total, vit_q.shape[1]), f32),
            pltpu.VMEM((total, width), f32),
            pltpu.VMEM((half, width), f32),
            pltpu.VMEM((devices, half // 2, 2 * width), bf16),
            pltpu.VMEM((token_count, cols), f32),
            pltpu.VMEM((token_count, cols), f32),
            pltpu.VMEM((pairs, text_count, 2 * key_cols), bf16),
            pltpu.VMEM((text_count, 2 * key_cols), f32),
            pltpu.VMEM((pairs, text_count, 2 * key_cols), bf16),
            pltpu.VMEM((pairs, owner_slots, 2 * key_cols + MARK), bf16),
            pltpu.VMEM((pairs, owner_slots, 2 * key_cols + MARK), bf16),
            pltpu.VMEM((pairs, owner_slots, 2 * key_cols + MARK), bf16),
            pltpu.VMEM((pairs, owner_slots, 2 * key_cols + MARK), bf16),
            pltpu.VMEM((owner_slots, 2 * key_cols + MARK), f32),
            dma((9,)),
            dma((2, devices)),
            dma((2, devices)),
            dma((2,)),
            dma((2, devices)),
            dma((2, cols // 256)),
            dma((2, devices)),
            dma((2, devices)),
            dma((2,)),
            dma((2, pairs)),
            dma((2, pairs)),
        ],
        compiler_params=pltpu.CompilerParams(
            collective_id=0, has_side_effects=True, vmem_limit_bytes=56 * 1024 * 1024
        ),
    )(
        patches,
        image_tokens,
        vit_gain,
        vit_q,
        vit_k,
        vit_v,
        vit_out,
        merge_gain,
        merger_out,
        text_rows,
        vis_route.reshape(-1),
        vis_seq,
        llm_gain,
        llm_k,
        llm_v,
    )
    segment = text_seg[0]
    positions = jnp.arange(text_count, dtype=jnp.int32)
    text_allowed = (segment[:, None] == segment[None, :]) & (
        positions[None, :] <= positions[:, None]
    )
    visual_allowed = visual_marker == (segment + 1)[:, None]
    allowed = jnp.concatenate([visual_allowed, text_allowed], axis=1)
    local_groups = key_cols // HD
    query_heads = text_query.reshape(text_count, local_groups, QH // KVH, HD)
    all_keys = pair[:, :key_cols].reshape(-1, local_groups, HD)
    all_values = pair[:, key_cols:].reshape(-1, local_groups, HD)
    return local_attention(query_heads, all_keys, all_values, allowed, 1.0 / math.sqrt(HD))


def solution(mesh):
    in_specs = (
        P(("groups", "dp"), None),
        P(("groups", "dp"), None),
        P(),
        P(None, "tensor"),
        P(None, "tensor"),
        P(None, "tensor"),
        P("tensor", None),
        P(),
        P("tensor", "dp"),
        P(("groups", "dp"), None),
        P(("groups", "dp"), "tensor"),
        P(("groups", "dp"), None),
        P("groups", None),
        P("groups"),
        P(),
        P("dp", "tensor"),
        P("dp", "tensor"),
    )
    out_specs = P(("groups", "dp"), "tensor")
    return jax.shard_map(body, mesh=mesh, in_specs=in_specs, out_specs=out_specs, check_vma=False)
```

```python
import functools
import math

import jax
import jax.numpy as jnp
from jax import lax
from jax.experimental import pallas as pl
from jax.experimental.pallas import tpu as pltpu
from jax.sharding import PartitionSpec as P

VHD = 80
QH = 32
KVH = 4
HD = 128


EPSILON = 1e-06
NEG_LARGE = -1e30


def layer_norm(values, scale_gain):
    values = values.astype(jnp.float32)
    centred = values - jnp.mean(values, axis=-1, keepdims=True)
    spread = jnp.mean(centred * centred, axis=-1, keepdims=True)
    return centred * lax.rsqrt(spread + EPSILON) * scale_gain


def local_attention(query, keys, values, allowed, scale):
    scores = jnp.einsum("tagd,kad->agtk", query, keys, preferred_element_type=jnp.float32) * scale
    scores = jnp.where(allowed[None, None], scores, NEG_LARGE)
    weights = jax.nn.softmax(scores, axis=-1).astype(jnp.bfloat16)
    mixed = jnp.einsum("agtk,kad->tagd", weights, values, preferred_element_type=jnp.float32)
    return mixed.reshape(query.shape[0], -1).astype(jnp.bfloat16)


MESH = pl.DeviceIdType.MESH
MARK = 128


def dot32(left, right):
    return jnp.dot(left, right, preferred_element_type=jnp.float32)


def kernel(
    n,
    patches,
    image_tokens,
    vit_gain,
    vit_q_hbm,
    vit_k_hbm,
    vit_v_hbm,
    vit_out_hbm,
    merge_gain,
    merger_hbm,
    text_hbm,
    route,
    vis_seq,
    llm_gain_flat,
    llm_k_hbm,
    llm_v_hbm,
    out,
    marker,
    code,
    llm_gain,
    ordered,
    wq,
    wk,
    wv,
    wo,
    merger,
    pair_weight,
    text,
    text_scale,
    route_wide,
    seq_wide,
    text_buf,
    query,
    keys,
    values,
    mixed,
    mix,
    mix_recv,
    merged,
    part,
    part_recv,
    text_send,
    text_sum,
    text_recv,
    vis_send,
    vis_recv,
    vis_mate,
    vis_mate_recv,
    vis_sum,
    load_sem,
    text_sems,
    forward_sems,
    mix_sems,
    merged_sems,
    part_sems,
    text_back_sems,
    vis_back_sems,
    weight_sems,
    twin_sems,
    mate_sems,
):
    me = lax.axis_index("dp")
    core = lax.axis_index("tensor")
    other = 1 - core
    rows = text_buf.shape[1]
    text_half = rows // 2
    cols = merger.shape[1]
    width = llm_gain.shape[1]
    nz = n // 2
    z, y = me // 2, lax.rem(me, 2)
    mate = {"dp": me + 1 - 2 * y}
    sibling = {"tensor": other}
    kv = llm_k_hbm.shape[1]

    def z_ahead(step):
        return lax.rem(z + step, nz)

    def z_behind(step):
        return lax.rem(z + nz - step, nz)

    mine = pl.ds(pl.multiple_of(core * text_half, text_half), text_half)
    theirs = pl.ds(pl.multiple_of(other * text_half, text_half), text_half)
    own_weight = pl.ds(pl.multiple_of(y * cols, cols), cols)
    loads = [
        pltpu.make_async_copy(source, target, load_sem.at[i])
        for i, (source, target) in enumerate(
            [
                (text_hbm, text),
                (vit_q_hbm, wq),
                (vit_k_hbm, wk),
                (vit_v_hbm, wv),
                (vit_out_hbm, wo),
                (llm_k_hbm, pair_weight.at[own_weight, 0:kv]),
                (llm_v_hbm, pair_weight.at[own_weight, kv : 2 * kv]),
                (merger_hbm, merger),
            ]
        )
    ]
    for load in loads:
        load.start()

    barrier = pltpu.get_barrier_semaphore()

    def greet(step, carry):
        peer = {"dp": z_ahead(step) * 2 + y}
        pl.semaphore_signal(barrier, inc=1, device_id=peer, device_id_type=MESH)
        return carry

    lax.fori_loop(1, nz, greet, 0)
    pl.semaphore_signal(barrier, inc=1, device_id=mate, device_id_type=MESH)
    pl.semaphore_signal(barrier, inc=1, device_id=sibling, device_id_type=MESH)

    def remote(source, target, send, recv, device):
        return pltpu.make_async_remote_copy(
            src_ref=source,
            dst_ref=target,
            send_sem=send,
            recv_sem=recv,
            device_id=device,
            device_id_type=MESH,
        )

    def text_copy(step):
        start = pl.multiple_of(z_ahead(step) * 2 * cols, 2 * cols)
        return remote(
            text_hbm.at[mine, pl.ds(start, 2 * cols)],
            text_buf.at[step, mine],
            text_sems.at[0, step],
            text_sems.at[1, step],
            {"dp": z_ahead(step) * 2 + y},
        )

    def forward_copy(step):
        return remote(
            text_buf.at[step, mine],
            text_buf.at[step, mine],
            forward_sems.at[0, step],
            forward_sems.at[1, step],
            sibling,
        )

    chunk = merged.shape[1] // 2

    def merged_copy(index):
        step = index // 2
        at = pl.ds(pl.multiple_of(lax.rem(index, 2) * chunk, chunk), chunk)
        return remote(
            merged.at[0, at],
            merged.at[2 * step, at],
            merged_sems.at[0, index],
            merged_sems.at[1, index],
            {"dp": z_ahead(step) * 2 + y},
        )

    def twin_copy(index):
        step = index // 2
        at = pl.ds(pl.multiple_of(lax.rem(index, 2) * chunk, chunk), chunk)
        return remote(
            merged.at[2 * step, at],
            merged.at[2 * step + 1, at],
            twin_sems.at[0, index],
            twin_sems.at[1, index],
            mate,
        )

    def weight_copy(i):
        piece = pair_weight.at[own_weight, i * kv : (i + 1) * kv]
        return remote(
            piece,
            piece,
            weight_sems.at[0, i],
            weight_sems.at[1, i],
            mate,
        )

    def text_back(step):
        return remote(
            text_send.at[step],
            text_recv.at[step],
            text_back_sems.at[0, step],
            text_back_sems.at[1, step],
            {"dp": z_behind(step) * 2 + y},
        )

    def vis_back(step):
        return remote(
            vis_send.at[step],
            vis_recv.at[step],
            vis_back_sems.at[0, step],
            vis_back_sems.at[1, step],
            {"dp": z_ahead(step) * 2 + y},
        )

    def mate_copy(step):
        return remote(
            vis_mate.at[step],
            vis_mate_recv.at[step],
            mate_sems.at[0, step],
            mate_sems.at[1, step],
            mate,
        )

    def each(first, last, act):
        def run(step, carry):
            act(step)
            return carry

        lax.fori_loop(first, last, run, 0)

    llm_gain[...] = llm_gain_flat[...].reshape(1, -1)

    own_cols = pl.ds(pl.multiple_of(z * 2 * cols, 2 * cols), 2 * cols)
    own_text = pltpu.make_async_copy(text_hbm.at[:, own_cols], text_buf.at[0], load_sem.at[8])
    own_text.start()
    pl.semaphore_wait(barrier, nz + 1)
    text_copy(nz // 2).start()
    loads[5].wait()
    weight_copy(0).start()

    count = patches.shape[0]
    quarter = count // 4

    def token_of(place):
        part_of = sum([(place >= j * quarter).astype(jnp.int32) for j in range(1, 4)])
        return place - quarter * part_of, part_of

    def image_at(place):
        token, end, image = token_of(place)[0], 0, 0
        for i in range(image_tokens.shape[1]):
            end = end + image_tokens[0, i]
            image = image + (token >= end).astype(jnp.int32)
        return image

    down = lax.broadcasted_iota(jnp.int32, (count, count), 0)
    across = lax.broadcasted_iota(jnp.int32, (count, count), 1)
    token, place = token_of(down)
    chosen = jnp.where(across == 4 * token + place, 1.0, 0.0).astype(jnp.bfloat16)
    ordered[...] = dot32(chosen, patches[...])

    normed = layer_norm(ordered[...], vit_gain[...].reshape(1, -1)).astype(jnp.bfloat16)
    for load, weight, place in zip(loads[1:4], (wq, wk, wv), (query, keys, values)):
        load.wait()
        place[...] = dot32(normed, weight[...]).astype(jnp.bfloat16)
    same = image_at(down) == image_at(across)
    mixed[...] = jnp.zeros_like(mixed)
    for head in range(query.shape[1] // VHD):
        low = head * VHD
        base = low // 128 * 128
        end = -(-(low + VHD) // 128) * 128
        lane = lax.broadcasted_iota(jnp.int32, (query.shape[0], end - base), 1)
        inside = (lane >= low - base) & (lane < low - base + VHD)
        q = jnp.where(inside, query[:, base:end].astype(jnp.float32), 0.0).astype(jnp.bfloat16)
        v = jnp.where(inside, values[:, base:end].astype(jnp.float32), 0.0).astype(jnp.bfloat16)
        scores = lax.dot_general(
            q, keys[:, base:end], (((1,), (1,)), ((), ())), preferred_element_type=jnp.float32
        ) * (1.0 / math.sqrt(VHD))
        scores = jnp.where(same, scores, NEG_LARGE)
        scores = jnp.exp(scores - jnp.max(scores, axis=1, keepdims=True))
        weights = (scores / jnp.sum(scores, axis=1, keepdims=True)).astype(jnp.bfloat16)
        mixed[:, base:end] += dot32(weights, v)
    loads[4].wait()
    mix[...] = dot32(mixed[...].astype(jnp.bfloat16), wo[...])
    half = mix.shape[0] // 2
    own_half = pl.ds(pl.multiple_of(core * half, half), half)
    other_half = pl.ds(pl.multiple_of(other * half, half), half)
    swap = remote(mix.at[other_half], mix_recv, mix_sems.at[0], mix_sems.at[1], sibling)
    swap.start()
    swap.wait()
    hidden = (ordered[own_half, :] + (mix[own_half, :] + mix_recv[...])).astype(
        jnp.bfloat16
    )
    normal = layer_norm(hidden, merge_gain[...].reshape(1, -1)).astype(jnp.bfloat16)
    vision_width = normal.shape[1]
    merged[0, :, 0:vision_width] = normal[: half // 2]
    merged[0, :, vision_width : 2 * vision_width] = normal[half // 2 :]
    each(1, nz, lambda step: merged_copy(2 * step).start())
    each(1, nz, lambda step: merged_copy(2 * step + 1).start())
    each(0, 2, lambda index: twin_copy(index).start())
    each(1, nz // 2, lambda step: text_copy(step).start())
    each(nz // 2 + 1, nz, lambda step: text_copy(step).start())

    route_wide[...] = jnp.broadcast_to(
        route[...].astype(jnp.float32).reshape(1, -1), (128, code.shape[0])
    ).T
    seq_wide[...] = jnp.broadcast_to(
        vis_seq[...].astype(jnp.float32).reshape(1, -1), (128, code.shape[0])
    ).T
    slots = vis_send.shape[1]
    per_block = code.shape[0] // n
    capacity = slots // n
    lanes = lax.broadcasted_iota(jnp.int32, (per_block, 128), 1)
    before = jnp.where(
        lax.broadcasted_iota(jnp.int32, (per_block, per_block), 1)
        < lax.broadcasted_iota(jnp.int32, (per_block, per_block), 0),
        1.0,
        0.0,
    ).astype(jnp.bfloat16)
    slot_of = lax.broadcasted_iota(jnp.int32, (per_block, slots), 1) + me * slots

    def place_block(i, total):
        parity = lax.rem(i, 2)
        source = z_behind(i // 2) * 2 + lax.rem(y + parity, 2)
        at = pl.ds(pl.multiple_of(source * per_block, per_block), per_block)
        owner = route_wide[at, :].astype(jnp.int32)
        onehot = jnp.where(lanes == owner, 1.0, 0.0)
        earlier = dot32(before, onehot.astype(jnp.bfloat16))
        rank = jnp.sum(earlier * onehot, axis=1, keepdims=True).astype(jnp.int32)
        number = owner[:, 0:1] * slots + source * capacity + rank
        code[pl.ds(pl.multiple_of(i * per_block, per_block), per_block), :] = number
        named = jnp.where(number == slot_of, seq_wide[at, 0:slots].astype(jnp.int32) + 1, 0)
        return total + jnp.sum(named, axis=0, keepdims=True)

    marker[...] = lax.fori_loop(0, n, place_block, jnp.zeros((1, slots), jnp.int32))

    def hand_over(step):
        text_copy(step).wait_recv()
        forward_copy(step).start()

    loads[0].wait()

    def scale_rows(i, carry):
        at = pl.ds(pl.multiple_of(i * 16, 16), 16)
        wide = text[at, :].astype(jnp.float32)
        squares = jnp.sum(wide * wide, axis=1, keepdims=True)
        text_scale[at, :] = jnp.broadcast_to(
            lax.rsqrt(squares / width + EPSILON), (16, text_scale.shape[1])
        )
        return carry

    lax.fori_loop(0, rows // 16, scale_rows, 0)

    def pass_on(index):
        merged_copy(index).wait_recv()
        twin_copy(index).start()

    each(1, nz, lambda step: pass_on(2 * step))
    each(1, nz, lambda step: pass_on(2 * step + 1))
    loads[6].wait()
    weight_copy(1).start()
    hand_over(nz // 2)

    loads[7].wait()
    each(0, 2 * nz, lambda index: twin_copy(index).wait_recv())
    gathered = merged[...].reshape(-1, merged.shape[2])
    block = 256

    def part_copy(i):
        at = pl.ds(pl.multiple_of(i * block, block), block)
        return remote(
            part.at[:, at], part_recv.at[:, at], part_sems.at[0, i], part_sems.at[1, i], sibling
        )

    for i in range(cols // block):
        at = slice(i * block, (i + 1) * block)
        part[:, at] = dot32(gathered, merger[:, at])
        part_copy(i).start()
    tokens = part.shape[0]
    power = jnp.zeros((tokens, 1), jnp.float32)
    pair = jnp.zeros((tokens, 2 * kv), jnp.float32)
    for i in range(cols // block):
        at = slice(i * block, (i + 1) * block)
        part_copy(i).wait_recv()
        wide = (part[:, at] + part_recv[:, at]).astype(jnp.bfloat16).astype(jnp.float32)
        power = power + jnp.sum(wide * wide, axis=1, keepdims=True)
        gain = llm_gain[:, pl.ds(pl.multiple_of(me * cols + i * block, block), block)]
        weight = pair_weight[pl.ds(pl.multiple_of(y * cols + i * block, block), block), :]
        pair = pair + dot32((wide * gain).astype(jnp.bfloat16), weight)

    def marked(square):
        coarse = square.astype(jnp.bfloat16).astype(jnp.float32)
        lane = lax.broadcasted_iota(jnp.int32, (square.shape[0], MARK), 1)
        return jnp.where(lane < MARK // 2, coarse, square - coarse).astype(jnp.bfloat16)

    row = jnp.concatenate([pair.astype(jnp.bfloat16), marked(power)], axis=1)

    def route_to(owner):
        wanted = lax.broadcasted_iota(jnp.int32, (tokens, slots), 1) + owner * slots
        picked = jnp.where(code[...] == wanted, 1.0, 0.0).astype(jnp.bfloat16)
        return lax.dot_general(
            picked, row, (((0,), (0,)), ((), ())), preferred_element_type=jnp.float32
        )

    def route_for_mate(step):
        vis_mate[step] = route_to(z_ahead(step) * 2 + 1 - y).astype(jnp.bfloat16)
        mate_copy(step).start()

    def route_own(step):
        total = route_to(z_ahead(step) * 2 + y)
        mate_copy(step).wait_recv()
        return total + vis_mate_recv[step].astype(jnp.float32)

    def route_and_send(step):
        total = route_own(step)
        square = jnp.sum(total[:, 2 * kv :], axis=1, keepdims=True) * (2.0 / MARK)
        vis_send[step, :, 0 : 2 * kv] = total[:, : 2 * kv].astype(jnp.bfloat16)
        vis_send[step, :, 2 * kv :] = marked(square)
        vis_back(step).start()

    each(1, nz, route_for_mate)
    route_for_mate(0)
    each(1, nz // 2, hand_over)
    each(nz // 2 + 1, nz, hand_over)
    each(1, nz, route_and_send)
    weight_copy(0).wait_recv()
    weight_copy(1).wait_recv()

    def project_text(step):
        gained = (text_buf[step].astype(jnp.float32) * llm_gain[:, own_cols]).astype(jnp.bfloat16)
        return dot32(gained, pair_weight[...])

    def project_and_send(step):
        forward_copy(step).wait_recv()
        text_send[step] = project_text(step).astype(jnp.bfloat16)
        text_back(step).start()

    project_and_send(nz // 2)
    each(1, nz // 2, project_and_send)
    each(nz // 2 + 1, nz, project_and_send)
    own_text.wait()
    text_sum[...] = project_text(0)
    vis_sum[...] = route_own(0)


    def add_text(step, total):
        text_back(step).wait_recv()
        return total + text_recv[step].astype(jnp.float32)

    text_total = lax.fori_loop(1, nz, add_text, text_sum[...])
    out[slots:, :] = (text_total * text_scale[:, 0:1]).astype(jnp.bfloat16)

    def add_visual(step, total):
        vis_back(step).wait_recv()
        return total + vis_recv[step].astype(jnp.float32)

    total = lax.fori_loop(1, nz, add_visual, vis_sum[...])
    squares = jnp.sum(total[:, 2 * kv :], axis=1, keepdims=True) * (2.0 / MARK)
    out[:slots, :] = (total[:, : 2 * kv] * lax.rsqrt(squares / width + EPSILON)).astype(jnp.bfloat16)

    each(1, nz, lambda step: forward_copy(step).wait_send())
    each(0, 2 * nz, lambda index: twin_copy(index).wait_send())
    weight_copy(0).wait_send()
    weight_copy(1).wait_send()
    for i in range(cols // block):
        part_copy(i).wait_send()

    def drain(step):
        text_copy(step).wait_send()
        merged_copy(2 * step).wait_send()
        merged_copy(2 * step + 1).wait_send()
        text_back(step).wait_send()

    each(1, nz, drain)
    each(1, nz, lambda step: vis_back(step).wait_send())
    each(0, nz, lambda step: mate_copy(step).wait_send())


def body(
    patches,
    image_tokens,
    vit_gain,
    vit_q,
    vit_k,
    vit_v,
    vit_out,
    merge_gain,
    merger_out,
    text_rows,
    text_query,
    text_seg,
    vis_route,
    vis_seq,
    llm_gain,
    llm_k,
    llm_v,
):
    devices = lax.axis_size("dp")
    total, width = patches.shape
    key_cols = llm_k.shape[1]
    token_count = vis_route.shape[0]
    owner_slots = 2 * token_count // devices
    text_count, model_width = text_rows.shape
    cols = merger_out.shape[1]
    half = total // 2
    vmem = pl.BlockSpec(memory_space=pltpu.VMEM)
    smem = pl.BlockSpec(memory_space=pltpu.SMEM)
    hbm = pl.BlockSpec(memory_space=pl.ANY)
    bf16, f32 = jnp.bfloat16, jnp.float32
    dma = pltpu.SemaphoreType.DMA
    pairs = devices // 2
    pair, visual_marker = pl.pallas_call(
        functools.partial(kernel, devices),
        out_shape=(
            jax.ShapeDtypeStruct((owner_slots + text_count, 2 * key_cols), bf16),
            jax.ShapeDtypeStruct((1, owner_slots), jnp.int32),
        ),
        in_specs=[vmem, smem, vmem] + [hbm] * 4 + [vmem, hbm, hbm, vmem, vmem, vmem, hbm, hbm],
        out_specs=(vmem, vmem),
        scratch_shapes=[
            pltpu.VMEM((token_count, 1), jnp.int32),
            pltpu.VMEM((1, model_width), f32),
            pltpu.VMEM((total, width), f32),
            pltpu.VMEM(vit_q.shape, bf16),
            pltpu.VMEM(vit_k.shape, bf16),
            pltpu.VMEM(vit_v.shape, bf16),
            pltpu.VMEM(vit_out.shape, bf16),
            pltpu.VMEM(merger_out.shape, bf16),
            pltpu.VMEM((2 * cols, 2 * key_cols), bf16),
            pltpu.VMEM((text_count, model_width), bf16),
            pltpu.VMEM((text_count, 128), f32),
            pltpu.VMEM((token_count, 128), f32),
            pltpu.VMEM((token_count, 128), f32),
            pltpu.VMEM((pairs, text_count, 2 * cols), bf16),
            pltpu.VMEM((total, vit_q.shape[1]), bf16),
            pltpu.VMEM((total, vit_q.shape[1]), bf16),
            pltpu.VMEM((total, vit_q.shape[1]), bf16),
            pltpu.VMEM((total, vit_q.shape[1]), f32),
            pltpu.VMEM((total, width), f32),
            pltpu.VMEM((half, width), f32),
            pltpu.VMEM((devices, half // 2, 2 * width), bf16),
            pltpu.VMEM((token_count, cols), f32),
            pltpu.VMEM((token_count, cols), f32),
            pltpu.VMEM((pairs, text_count, 2 * key_cols), bf16),
            pltpu.VMEM((text_count, 2 * key_cols), f32),
            pltpu.VMEM((pairs, text_count, 2 * key_cols), bf16),
            pltpu.VMEM((pairs, owner_slots, 2 * key_cols + MARK), bf16),
            pltpu.VMEM((pairs, owner_slots, 2 * key_cols + MARK), bf16),
            pltpu.VMEM((pairs, owner_slots, 2 * key_cols + MARK), bf16),
            pltpu.VMEM((pairs, owner_slots, 2 * key_cols + MARK), bf16),
            pltpu.VMEM((owner_slots, 2 * key_cols + MARK), f32),
            dma((9,)),
            dma((2, devices)),
            dma((2, devices)),
            dma((2,)),
            dma((2, 2 * pairs)),
            dma((2, cols // 256)),
            dma((2, devices)),
            dma((2, devices)),
            dma((2, 2)),
            dma((2, 2 * pairs)),
            dma((2, pairs)),
        ],
        compiler_params=pltpu.CompilerParams(
            collective_id=0, has_side_effects=True, vmem_limit_bytes=56 * 1024 * 1024
        ),
    )(
        patches,
        image_tokens,
        vit_gain,
        vit_q,
        vit_k,
        vit_v,
        vit_out,
        merge_gain,
        merger_out,
        text_rows,
        vis_route.reshape(-1),
        vis_seq,
        llm_gain,
        llm_k,
        llm_v,
    )
    segment = text_seg[0]
    positions = jnp.arange(text_count, dtype=jnp.int32)
    text_allowed = (segment[:, None] == segment[None, :]) & (
        positions[None, :] <= positions[:, None]
    )
    visual_allowed = visual_marker == (segment + 1)[:, None]
    allowed = jnp.concatenate([visual_allowed, text_allowed], axis=1)
    local_groups = key_cols // HD
    query_heads = text_query.reshape(text_count, local_groups, QH // KVH, HD)
    all_keys = pair[:, :key_cols].reshape(-1, local_groups, HD)
    all_values = pair[:, key_cols:].reshape(-1, local_groups, HD)
    return local_attention(query_heads, all_keys, all_values, allowed, 1.0 / math.sqrt(HD))


def solution(mesh):
    in_specs = (
        P(("groups", "dp"), None),
        P(("groups", "dp"), None),
        P(),
        P(None, "tensor"),
        P(None, "tensor"),
        P(None, "tensor"),
        P("tensor", None),
        P(),
        P("tensor", "dp"),
        P(("groups", "dp"), None),
        P(("groups", "dp"), "tensor"),
        P(("groups", "dp"), None),
        P("groups", None),
        P("groups"),
        P(),
        P("dp", "tensor"),
        P("dp", "tensor"),
    )
    out_specs = P(("groups", "dp"), "tensor")
    return jax.shard_map(body, mesh=mesh, in_specs=in_specs, out_specs=out_specs, check_vma=False)
```

```python
import functools
import math

import jax
import jax.numpy as jnp
from jax import lax
from jax.experimental import pallas as pl
from jax.experimental.pallas import tpu as pltpu
from jax.sharding import PartitionSpec as P

VHD = 80
QH = 32
KVH = 4
HD = 128


EPSILON = 1e-06
NEG_LARGE = -1e30


def layer_norm(values, scale_gain):
    values = values.astype(jnp.float32)
    centred = values - jnp.mean(values, axis=-1, keepdims=True)
    spread = jnp.mean(centred * centred, axis=-1, keepdims=True)
    return centred * lax.rsqrt(spread + EPSILON) * scale_gain


def local_attention(query, keys, values, allowed, scale):
    scores = jnp.einsum("tagd,kad->agtk", query, keys, preferred_element_type=jnp.float32) * scale
    scores = jnp.where(allowed[None, None], scores, NEG_LARGE)
    weights = jax.nn.softmax(scores, axis=-1).astype(jnp.bfloat16)
    mixed = jnp.einsum("agtk,kad->tagd", weights, values, preferred_element_type=jnp.float32)
    return mixed.reshape(query.shape[0], -1).astype(jnp.bfloat16)


MESH = pl.DeviceIdType.MESH
MARK = 128


def dot32(left, right):
    return jnp.dot(left, right, preferred_element_type=jnp.float32)


def kernel(
    n,
    patches,
    image_tokens,
    vit_gain,
    vit_q_hbm,
    vit_k_hbm,
    vit_v_hbm,
    vit_out_hbm,
    merge_gain,
    merger_hbm,
    text_hbm,
    route,
    vis_seq,
    llm_gain_flat,
    llm_k_hbm,
    llm_v_hbm,
    out,
    marker,
    code,
    llm_gain,
    ordered,
    wq,
    wk,
    wv,
    wo,
    merger,
    pair_weight,
    text,
    text_scale,
    route_wide,
    seq_wide,
    text_buf,
    query,
    keys,
    values,
    mixed,
    mix,
    mix_recv,
    merged,
    part,
    part_recv,
    text_send,
    text_sum,
    text_recv,
    vis_send,
    vis_recv,
    vis_mate,
    vis_mate_recv,
    vis_sum,
    load_sem,
    text_sems,
    forward_sems,
    mix_sems,
    merged_sems,
    part_sems,
    text_back_sems,
    vis_back_sems,
    weight_sems,
    twin_sems,
    mate_sems,
):
    me = lax.axis_index("dp")
    core = lax.axis_index("tensor")
    other = 1 - core
    rows = text_buf.shape[1]
    text_half = rows // 2
    cols = merger.shape[1]
    width = llm_gain.shape[1]
    nz = n // 2
    z, y = me // 2, lax.rem(me, 2)
    mate = {"dp": me + 1 - 2 * y}
    sibling = {"tensor": other}
    kv = llm_k_hbm.shape[1]

    def z_ahead(step):
        return lax.rem(z + step, nz)

    def z_behind(step):
        return lax.rem(z + nz - step, nz)

    mine = pl.ds(pl.multiple_of(core * text_half, text_half), text_half)
    theirs = pl.ds(pl.multiple_of(other * text_half, text_half), text_half)
    own_weight = pl.ds(pl.multiple_of(y * cols, cols), cols)
    loads = [
        pltpu.make_async_copy(source, target, load_sem.at[i])
        for i, (source, target) in enumerate(
            [
                (text_hbm, text),
                (vit_q_hbm, wq),
                (vit_k_hbm, wk),
                (vit_v_hbm, wv),
                (vit_out_hbm, wo),
                (llm_k_hbm, pair_weight.at[own_weight, 0:kv]),
                (llm_v_hbm, pair_weight.at[own_weight, kv : 2 * kv]),
                (merger_hbm, merger),
            ]
        )
    ]
    for load in loads:
        load.start()

    barrier = pltpu.get_barrier_semaphore()

    def greet(step, carry):
        peer = {"dp": z_ahead(step) * 2 + y}
        pl.semaphore_signal(barrier, inc=1, device_id=peer, device_id_type=MESH)
        return carry

    lax.fori_loop(1, nz, greet, 0)
    pl.semaphore_signal(barrier, inc=1, device_id=mate, device_id_type=MESH)
    pl.semaphore_signal(barrier, inc=1, device_id=sibling, device_id_type=MESH)

    def remote(source, target, send, recv, device):
        return pltpu.make_async_remote_copy(
            src_ref=source,
            dst_ref=target,
            send_sem=send,
            recv_sem=recv,
            device_id=device,
            device_id_type=MESH,
        )

    def text_copy(step):
        start = pl.multiple_of(z_ahead(step) * 2 * cols, 2 * cols)
        return remote(
            text_hbm.at[mine, pl.ds(start, 2 * cols)],
            text_buf.at[step, mine],
            text_sems.at[0, step],
            text_sems.at[1, step],
            {"dp": z_ahead(step) * 2 + y},
        )

    def forward_copy(step):
        return remote(
            text_buf.at[step, mine],
            text_buf.at[step, mine],
            forward_sems.at[0, step],
            forward_sems.at[1, step],
            sibling,
        )

    def merged_copy(step):
        return remote(
            merged.at[0],
            merged.at[2 * step],
            merged_sems.at[0, step],
            merged_sems.at[1, step],
            {"dp": z_ahead(step) * 2 + y},
        )

    def twin_copy(step):
        return remote(
            merged.at[2 * step],
            merged.at[2 * step + 1],
            twin_sems.at[0, step],
            twin_sems.at[1, step],
            mate,
        )

    def weight_copy():
        return remote(
            pair_weight.at[own_weight],
            pair_weight.at[own_weight],
            weight_sems.at[0],
            weight_sems.at[1],
            mate,
        )

    def text_back(step):
        return remote(
            text_send.at[step],
            text_recv.at[step],
            text_back_sems.at[0, step],
            text_back_sems.at[1, step],
            {"dp": z_behind(step) * 2 + y},
        )

    def vis_back(step):
        return remote(
            vis_send.at[step],
            vis_recv.at[step],
            vis_back_sems.at[0, step],
            vis_back_sems.at[1, step],
            {"dp": z_ahead(step) * 2 + y},
        )

    def mate_copy(step):
        return remote(
            vis_mate.at[step],
            vis_mate_recv.at[step],
            mate_sems.at[0, step],
            mate_sems.at[1, step],
            mate,
        )

    def each(first, last, act):
        def run(step, carry):
            act(step)
            return carry

        lax.fori_loop(first, last, run, 0)

    llm_gain[...] = llm_gain_flat[...].reshape(1, -1)

    own_cols = pl.ds(pl.multiple_of(z * 2 * cols, 2 * cols), 2 * cols)
    own_text = pltpu.make_async_copy(text_hbm.at[:, own_cols], text_buf.at[0], load_sem.at[8])
    own_text.start()
    pl.semaphore_wait(barrier, nz + 1)
    each(1, nz, lambda step: text_copy(step).start())
    loads[5].wait()
    loads[6].wait()
    weight_copy().start()

    count = patches.shape[0]
    quarter = count // 4

    def token_of(place):
        part_of = sum([(place >= j * quarter).astype(jnp.int32) for j in range(1, 4)])
        return place - quarter * part_of, part_of

    def image_at(place):
        token, end, image = token_of(place)[0], 0, 0
        for i in range(image_tokens.shape[1]):
            end = end + image_tokens[0, i]
            image = image + (token >= end).astype(jnp.int32)
        return image

    down = lax.broadcasted_iota(jnp.int32, (count, count), 0)
    across = lax.broadcasted_iota(jnp.int32, (count, count), 1)
    token, place = token_of(down)
    chosen = jnp.where(across == 4 * token + place, 1.0, 0.0).astype(jnp.bfloat16)
    ordered[...] = dot32(chosen, patches[...])

    normed = layer_norm(ordered[...], vit_gain[...].reshape(1, -1)).astype(jnp.bfloat16)
    for load, weight, place in zip(loads[1:4], (wq, wk, wv), (query, keys, values)):
        load.wait()
        place[...] = dot32(normed, weight[...]).astype(jnp.bfloat16)
    same = image_at(down) == image_at(across)
    mixed[...] = jnp.zeros_like(mixed)
    for head in range(query.shape[1] // VHD):
        low = head * VHD
        base = low // 128 * 128
        end = -(-(low + VHD) // 128) * 128
        lane = lax.broadcasted_iota(jnp.int32, (query.shape[0], end - base), 1)
        inside = (lane >= low - base) & (lane < low - base + VHD)
        q = jnp.where(inside, query[:, base:end].astype(jnp.float32), 0.0).astype(jnp.bfloat16)
        v = jnp.where(inside, values[:, base:end].astype(jnp.float32), 0.0).astype(jnp.bfloat16)
        scores = lax.dot_general(
            q, keys[:, base:end], (((1,), (1,)), ((), ())), preferred_element_type=jnp.float32
        ) * (1.0 / math.sqrt(VHD))
        scores = jnp.where(same, scores, NEG_LARGE)
        scores = jnp.exp(scores - jnp.max(scores, axis=1, keepdims=True))
        weights = (scores / jnp.sum(scores, axis=1, keepdims=True)).astype(jnp.bfloat16)
        mixed[:, base:end] += dot32(weights, v)
    loads[4].wait()
    mix[...] = dot32(mixed[...].astype(jnp.bfloat16), wo[...])
    half = mix.shape[0] // 2
    own_half = pl.ds(pl.multiple_of(core * half, half), half)
    other_half = pl.ds(pl.multiple_of(other * half, half), half)
    swap = remote(mix.at[other_half], mix_recv, mix_sems.at[0], mix_sems.at[1], sibling)
    swap.start()
    swap.wait()
    hidden = (ordered[own_half, :] + (mix[own_half, :] + mix_recv[...])).astype(
        jnp.bfloat16
    )
    normal = layer_norm(hidden, merge_gain[...].reshape(1, -1)).astype(jnp.bfloat16)
    vision_width = normal.shape[1]
    merged[0, :, 0:vision_width] = normal[: half // 2]
    merged[0, :, vision_width : 2 * vision_width] = normal[half // 2 :]
    each(1, nz, lambda step: merged_copy(step).start())
    twin_copy(0).start()

    route_wide[...] = jnp.broadcast_to(
        route[...].astype(jnp.float32).reshape(1, -1), (128, code.shape[0])
    ).T
    seq_wide[...] = jnp.broadcast_to(
        vis_seq[...].astype(jnp.float32).reshape(1, -1), (128, code.shape[0])
    ).T
    slots = vis_send.shape[1]
    per_block = code.shape[0] // n
    capacity = slots // n
    lanes = lax.broadcasted_iota(jnp.int32, (per_block, 128), 1)
    before = jnp.where(
        lax.broadcasted_iota(jnp.int32, (per_block, per_block), 1)
        < lax.broadcasted_iota(jnp.int32, (per_block, per_block), 0),
        1.0,
        0.0,
    ).astype(jnp.bfloat16)
    slot_of = lax.broadcasted_iota(jnp.int32, (per_block, slots), 1) + me * slots

    def place_block(i, total):
        parity = lax.rem(i, 2)
        source = z_behind(i // 2) * 2 + lax.rem(y + parity, 2)
        at = pl.ds(pl.multiple_of(source * per_block, per_block), per_block)
        owner = route_wide[at, :].astype(jnp.int32)
        onehot = jnp.where(lanes == owner, 1.0, 0.0)
        earlier = dot32(before, onehot.astype(jnp.bfloat16))
        rank = jnp.sum(earlier * onehot, axis=1, keepdims=True).astype(jnp.int32)
        number = owner[:, 0:1] * slots + source * capacity + rank
        code[pl.ds(pl.multiple_of(i * per_block, per_block), per_block), :] = number
        named = jnp.where(number == slot_of, seq_wide[at, 0:slots].astype(jnp.int32) + 1, 0)
        return total + jnp.sum(named, axis=0, keepdims=True)

    marker[...] = lax.fori_loop(0, n, place_block, jnp.zeros((1, slots), jnp.int32))

    def hand_over(step):
        text_copy(step).wait_recv()
        forward_copy(step).start()

    loads[0].wait()

    def scale_rows(i, carry):
        at = pl.ds(pl.multiple_of(i * 16, 16), 16)
        wide = text[at, :].astype(jnp.float32)
        squares = jnp.sum(wide * wide, axis=1, keepdims=True)
        text_scale[at, :] = jnp.broadcast_to(
            lax.rsqrt(squares / width + EPSILON), (16, text_scale.shape[1])
        )
        return carry

    lax.fori_loop(0, rows // 16, scale_rows, 0)

    def pass_on(step):
        merged_copy(step).wait_recv()
        twin_copy(step).start()

    each(1, nz, pass_on)
    each(1, nz, hand_over)
    weight_copy().wait_recv()

    def project_text(step):
        gained = (text_buf[step].astype(jnp.float32) * llm_gain[:, own_cols]).astype(jnp.bfloat16)
        return dot32(gained, pair_weight[...])

    def project_and_send(step):
        forward_copy(step).wait_recv()
        text_send[step] = project_text(step).astype(jnp.bfloat16)
        text_back(step).start()

    each(1, nz, project_and_send)
    own_text.wait()
    text_sum[...] = project_text(0)

    loads[7].wait()
    each(0, nz, lambda step: twin_copy(step).wait_recv())
    gathered = merged[...].reshape(-1, merged.shape[2])
    block = 256

    def part_copy(i):
        at = pl.ds(pl.multiple_of(i * block, block), block)
        return remote(
            part.at[:, at], part_recv.at[:, at], part_sems.at[0, i], part_sems.at[1, i], sibling
        )

    for i in range(cols // block):
        at = slice(i * block, (i + 1) * block)
        part[:, at] = dot32(gathered, merger[:, at])
        part_copy(i).start()
    tokens = part.shape[0]
    power = jnp.zeros((tokens, 1), jnp.float32)
    pair = jnp.zeros((tokens, 2 * kv), jnp.float32)
    for i in range(cols // block):
        at = slice(i * block, (i + 1) * block)
        part_copy(i).wait_recv()
        wide = (part[:, at] + part_recv[:, at]).astype(jnp.bfloat16).astype(jnp.float32)
        power = power + jnp.sum(wide * wide, axis=1, keepdims=True)
        gain = llm_gain[:, pl.ds(pl.multiple_of(me * cols + i * block, block), block)]
        weight = pair_weight[pl.ds(pl.multiple_of(y * cols + i * block, block), block), :]
        pair = pair + dot32((wide * gain).astype(jnp.bfloat16), weight)

    def marked(square):
        coarse = square.astype(jnp.bfloat16).astype(jnp.float32)
        lane = lax.broadcasted_iota(jnp.int32, (square.shape[0], MARK), 1)
        return jnp.where(lane < MARK // 2, coarse, square - coarse).astype(jnp.bfloat16)

    row = jnp.concatenate([pair.astype(jnp.bfloat16), marked(power)], axis=1)

    def route_to(owner):
        wanted = lax.broadcasted_iota(jnp.int32, (tokens, slots), 1) + owner * slots
        picked = jnp.where(code[...] == wanted, 1.0, 0.0).astype(jnp.bfloat16)
        return lax.dot_general(
            picked, row, (((0,), (0,)), ((), ())), preferred_element_type=jnp.float32
        )

    def route_for_mate(step):
        vis_mate[step] = route_to(z_ahead(step) * 2 + 1 - y).astype(jnp.bfloat16)
        mate_copy(step).start()

    def route_own(step):
        total = route_to(z_ahead(step) * 2 + y)
        mate_copy(step).wait_recv()
        return total + vis_mate_recv[step].astype(jnp.float32)

    def route_and_send(step):
        total = route_own(step)
        square = jnp.sum(total[:, 2 * kv :], axis=1, keepdims=True) * (2.0 / MARK)
        vis_send[step, :, 0 : 2 * kv] = total[:, : 2 * kv].astype(jnp.bfloat16)
        vis_send[step, :, 2 * kv :] = marked(square)
        vis_back(step).start()

    each(1, nz, route_for_mate)
    route_for_mate(0)
    each(1, nz, route_and_send)
    vis_sum[...] = route_own(0)


    def add_text(step, total):
        text_back(step).wait_recv()
        return total + text_recv[step].astype(jnp.float32)

    text_total = lax.fori_loop(1, nz, add_text, text_sum[...])
    out[slots:, :] = (text_total * text_scale[:, 0:1]).astype(jnp.bfloat16)

    def add_visual(step, total):
        vis_back(step).wait_recv()
        return total + vis_recv[step].astype(jnp.float32)

    total = lax.fori_loop(1, nz, add_visual, vis_sum[...])
    squares = jnp.sum(total[:, 2 * kv :], axis=1, keepdims=True) * (2.0 / MARK)
    out[:slots, :] = (total[:, : 2 * kv] * lax.rsqrt(squares / width + EPSILON)).astype(jnp.bfloat16)

    each(1, nz, lambda step: forward_copy(step).wait_send())
    each(0, nz, lambda step: twin_copy(step).wait_send())
    weight_copy().wait_send()
    for i in range(cols // block):
        part_copy(i).wait_send()

    def drain(step):
        text_copy(step).wait_send()
        merged_copy(step).wait_send()
        text_back(step).wait_send()

    each(1, nz, drain)
    each(1, nz, lambda step: vis_back(step).wait_send())
    each(0, nz, lambda step: mate_copy(step).wait_send())


def body(
    patches,
    image_tokens,
    vit_gain,
    vit_q,
    vit_k,
    vit_v,
    vit_out,
    merge_gain,
    merger_out,
    text_rows,
    text_query,
    text_seg,
    vis_route,
    vis_seq,
    llm_gain,
    llm_k,
    llm_v,
):
    devices = lax.axis_size("dp")
    total, width = patches.shape
    key_cols = llm_k.shape[1]
    token_count = vis_route.shape[0]
    owner_slots = 2 * token_count // devices
    text_count, model_width = text_rows.shape
    cols = merger_out.shape[1]
    half = total // 2
    vmem = pl.BlockSpec(memory_space=pltpu.VMEM)
    smem = pl.BlockSpec(memory_space=pltpu.SMEM)
    hbm = pl.BlockSpec(memory_space=pl.ANY)
    bf16, f32 = jnp.bfloat16, jnp.float32
    dma = pltpu.SemaphoreType.DMA
    pairs = devices // 2
    pair, visual_marker = pl.pallas_call(
        functools.partial(kernel, devices),
        out_shape=(
            jax.ShapeDtypeStruct((owner_slots + text_count, 2 * key_cols), bf16),
            jax.ShapeDtypeStruct((1, owner_slots), jnp.int32),
        ),
        in_specs=[vmem, smem, vmem] + [hbm] * 4 + [vmem, hbm, hbm, vmem, vmem, vmem, hbm, hbm],
        out_specs=(vmem, vmem),
        scratch_shapes=[
            pltpu.VMEM((token_count, 1), jnp.int32),
            pltpu.VMEM((1, model_width), f32),
            pltpu.VMEM((total, width), f32),
            pltpu.VMEM(vit_q.shape, bf16),
            pltpu.VMEM(vit_k.shape, bf16),
            pltpu.VMEM(vit_v.shape, bf16),
            pltpu.VMEM(vit_out.shape, bf16),
            pltpu.VMEM(merger_out.shape, bf16),
            pltpu.VMEM((2 * cols, 2 * key_cols), bf16),
            pltpu.VMEM((text_count, model_width), bf16),
            pltpu.VMEM((text_count, 128), f32),
            pltpu.VMEM((token_count, 128), f32),
            pltpu.VMEM((token_count, 128), f32),
            pltpu.VMEM((pairs, text_count, 2 * cols), bf16),
            pltpu.VMEM((total, vit_q.shape[1]), bf16),
            pltpu.VMEM((total, vit_q.shape[1]), bf16),
            pltpu.VMEM((total, vit_q.shape[1]), bf16),
            pltpu.VMEM((total, vit_q.shape[1]), f32),
            pltpu.VMEM((total, width), f32),
            pltpu.VMEM((half, width), f32),
            pltpu.VMEM((devices, half // 2, 2 * width), bf16),
            pltpu.VMEM((token_count, cols), f32),
            pltpu.VMEM((token_count, cols), f32),
            pltpu.VMEM((pairs, text_count, 2 * key_cols), bf16),
            pltpu.VMEM((text_count, 2 * key_cols), f32),
            pltpu.VMEM((pairs, text_count, 2 * key_cols), bf16),
            pltpu.VMEM((pairs, owner_slots, 2 * key_cols + MARK), bf16),
            pltpu.VMEM((pairs, owner_slots, 2 * key_cols + MARK), bf16),
            pltpu.VMEM((pairs, owner_slots, 2 * key_cols + MARK), bf16),
            pltpu.VMEM((pairs, owner_slots, 2 * key_cols + MARK), bf16),
            pltpu.VMEM((owner_slots, 2 * key_cols + MARK), f32),
            dma((9,)),
            dma((2, devices)),
            dma((2, devices)),
            dma((2,)),
            dma((2, devices)),
            dma((2, cols // 256)),
            dma((2, devices)),
            dma((2, devices)),
            dma((2,)),
            dma((2, pairs)),
            dma((2, pairs)),
        ],
        compiler_params=pltpu.CompilerParams(
            collective_id=0, has_side_effects=True, vmem_limit_bytes=56 * 1024 * 1024
        ),
    )(
        patches,
        image_tokens,
        vit_gain,
        vit_q,
        vit_k,
        vit_v,
        vit_out,
        merge_gain,
        merger_out,
        text_rows,
        vis_route.reshape(-1),
        vis_seq,
        llm_gain,
        llm_k,
        llm_v,
    )
    segment = text_seg[0]
    positions = jnp.arange(text_count, dtype=jnp.int32)
    text_allowed = (segment[:, None] == segment[None, :]) & (
        positions[None, :] <= positions[:, None]
    )
    visual_allowed = visual_marker == (segment + 1)[:, None]
    allowed = jnp.concatenate([visual_allowed, text_allowed], axis=1)
    local_groups = key_cols // HD
    query_heads = text_query.reshape(text_count, local_groups, QH // KVH, HD)
    all_keys = pair[:, :key_cols].reshape(-1, local_groups, HD)
    all_values = pair[:, key_cols:].reshape(-1, local_groups, HD)
    return local_attention(query_heads, all_keys, all_values, allowed, 1.0 / math.sqrt(HD))


def solution(mesh):
    in_specs = (
        P(("groups", "dp"), None),
        P(("groups", "dp"), None),
        P(),
        P(None, "tensor"),
        P(None, "tensor"),
        P(None, "tensor"),
        P("tensor", None),
        P(),
        P("tensor", "dp"),
        P(("groups", "dp"), None),
        P(("groups", "dp"), "tensor"),
        P(("groups", "dp"), None),
        P("groups", None),
        P("groups"),
        P(),
        P("dp", "tensor"),
        P("dp", "tensor"),
    )
    out_specs = P(("groups", "dp"), "tensor")
    return jax.shard_map(body, mesh=mesh, in_specs=in_specs, out_specs=out_specs, check_vma=False)
```
